256 devices in a mesh: tm: 16 (over x_hi, y, core), space: 16 (over x_lo, z).
Axes of the slice: x: 4 (x_hi: 2, x_lo: 2; x = x_hi * 2 + x_lo), y: 4, z: 8, core: 2. Of those that a mesh axis runs over, the one named last changes fastest.
Arguments:
- frames_in: bfloat16 [32, 32, 128, 256], P('tm', 'space'), may hold values from -6 to 6
- weight: bfloat16 [3, 3, 3, 256, 256], replicated, may hold values from -0.078125 to 0.078125
- cotangent: bfloat16 [32, 32, 128, 256], P('tm', 'space'), may hold values from -6 to 6
Outputs:
- output: bfloat16 [32, 32, 128, 256], P('tm', 'space')
- grad_input: bfloat16 [32, 32, 128, 256], P('tm', 'space')
- grad_weight: float32 [256, 3, 3, 3, 256], P('space')
The draws below stay inside these ranges and needn't reach their ends.
All inputs are finite; a program needn't handle non-finite values.
Results may differ from the reference program's by a relative error of at most 0.0032.
Values may be sent and summed in bfloat16 or wider, within the bound.
No kernel may reach another device: no remote copies, remote signals or barrier semaphores. Data moves between devices by JAX's collectives and lax.ppermute only.
A program may use at most 128 MiB of HBM per device.

```python
import jax
import jax.numpy as jnp
from jax import lax

CHANNELS = 256
WIDTH = 128
FRAMES = 32
HEIGHT = 32


def level_of(rng, extent, shards, least, high):
    level, own = 1.0, jax.random.fold_in(rng, 6)
    for axis_at, parts in shards:
        draws = jnp.exp(jax.random.uniform(jax.random.fold_in(own, axis_at), (parts,), jnp.float32, least / len(shards), high / len(shards)))
        level = level * jnp.repeat(draws, extent[axis_at] // parts).reshape([-1 if axis == axis_at else 1 for axis in range(len(extent))])
    return level


def normal_values(rng, extent, spread, reach, pieces=(), held_as=jnp.bfloat16):
    level = level_of(rng, extent, pieces, -0.22, 0.18) if pieces else 1.0
    result = jax.random.normal(rng, extent, jnp.float32) * spread * level
    return jnp.minimum(jnp.maximum(result, -reach), reach).astype(held_as)


def setup_inputs(seed: int = 0) -> dict:
    keys = jax.random.split(jax.random.key(seed), 4)
    return {
        "frames_in": normal_values(keys[0], (FRAMES, HEIGHT, WIDTH, CHANNELS), 1.0, 6.0, ((0, 16), (1, 16))),
        "weight": normal_values(keys[1], (3, 3, 3, CHANNELS, CHANNELS), (27 * CHANNELS) ** -0.5, 0.078125),
        "cotangent": normal_values(keys[2], (FRAMES, HEIGHT, WIDTH, CHANNELS), 1.0, 6.0, ((0, 16), (1, 16))),
    }


def unfold_cols(slab, offsets, count):
    return jnp.concatenate([slab[:, shift_c:shift_c + count] for shift_c in offsets], axis=-1)

def reference(frames_in, weight, cotangent):
    total_f, height, width, chans = frames_in.shape
    padded = jnp.pad(frames_in, ((2, 0), (1, 1), (1, 1), (0, 0)))
    fwd_mats = weight.reshape(3, 3, 3 * chans, chans)
    back_mats = jnp.transpose(weight, (0, 1, 2, 4, 3)).reshape(3, 3, 3 * chans, chans)
    frame_ids = jnp.arange(total_f, dtype=jnp.int32)

    def forward_frame(frame):
        block = lax.dynamic_slice_in_dim(padded, frame, 3, 0)
        acc = jnp.zeros((height * width, chans), jnp.float32)
        for tap_t in range(3):
            for tap_h in range(3):
                slab = block[tap_t, tap_h:tap_h + height]
                piece = unfold_cols(slab, (0, 1, 2), width).reshape(height * width, 3 * chans)
                acc = acc + jnp.dot(piece, fwd_mats[tap_t, tap_h], preferred_element_type=jnp.float32)
        return acc.reshape(height, width, chans)
    preact = lax.map(forward_frame, frame_ids)
    output = (frames_in.astype(jnp.float32) + jax.nn.silu(preact)).astype(jnp.bfloat16)
    sigma = jax.nn.sigmoid(preact)
    grad_pre = (cotangent.astype(jnp.float32) * sigma * (1.0 + preact * (1.0 - sigma))).astype(jnp.bfloat16)
    grad_pad = jnp.pad(grad_pre, ((0, 2), (1, 1), (1, 1), (0, 0)))

    def backward_frame(frame):
        block = lax.dynamic_slice_in_dim(grad_pad, frame, 3, 0)
        acc = jnp.zeros((height * width, chans), jnp.float32)
        for tap_t in range(3):
            for tap_h in range(3):
                slab = block[2 - tap_t, 2 - tap_h:2 - tap_h + height]
                piece = unfold_cols(slab, (2, 1, 0), width).reshape(height * width, 3 * chans)
                acc = acc + jnp.dot(piece, back_mats[tap_t, tap_h], preferred_element_type=jnp.float32)
        return acc.reshape(height, width, chans)
    back_sum = lax.map(backward_frame, frame_ids)
    grad_input = (cotangent.astype(jnp.float32) + back_sum).astype(jnp.bfloat16)

    def weight_step(carry, frame):
        block = lax.dynamic_slice_in_dim(padded, frame, 3, 0)
        grad_rows = lax.dynamic_index_in_dim(grad_pre, frame, 0, keepdims=False).reshape(height * width, chans)
        terms = []
        for tap_t in range(3):
            for tap_h in range(3):
                slab = block[tap_t, tap_h:tap_h + height]
                piece = unfold_cols(slab, (0, 1, 2), width).reshape(height * width, 3 * chans)
                terms.append(lax.dot_general(grad_rows, piece, (((0,), (0,)), ((), ())), preferred_element_type=jnp.float32))
        return (carry + jnp.concatenate(terms, axis=1), None)
    start = jnp.zeros((chans, 27 * chans), jnp.float32)
    summed, _ = lax.scan(weight_step, start, frame_ids)
    scale = 1.0 / jnp.sqrt(jnp.float32(total_f * height * width))
    grad_weight = (summed * scale).reshape(chans, 3, 3, 3, chans)
    return (output, grad_input, grad_weight)
```

```python
import functools
import itertools
import math

import jax
import jax.numpy as jnp
import numpy as np
from jax import lax
from jax.experimental import pallas as pl
from jax.experimental.pallas import tpu as pltpu
from jax.sharding import PartitionSpec as P

BOTH = ("tm", "space")
VMEM = pltpu.CompilerParams(vmem_limit_bytes=48 * 1024 * 1024)
SIZES = {"x_hi": 2, "y": 4, "core": 2, "x_lo": 2, "z": 8}


def groups_of(names):
    rest = [n for n in SIZES if n not in names]
    groups = []
    for fixed in itertools.product(*(range(SIZES[n]) for n in rest)):
        group = []
        for varied in itertools.product(*(range(SIZES[n]) for n in names)):
            at = dict(zip(rest, fixed)) | dict(zip(names, varied))
            tm = (at["x_hi"] * 4 + at["y"]) * 2 + at["core"]
            group.append(tm * 16 + at["x_lo"] * 8 + at["z"])
        groups.append(group)
    return groups


def exchange(value, names):
    return lax.all_to_all(value, BOTH, 0, 0, tiled=True, axis_index_groups=groups_of(names))


def flip_core(value):
    return lax.ppermute(value, "tm", [(i, i ^ 1) for i in range(16)])


def shifted(value, axis, steps):
    count = lax.axis_size(axis)
    leading, last = (max(0, -steps), min(count, count - steps))
    return lax.ppermute(value, axis, [(source, source + steps) for source in range(leading, last)])


def with_rows(x):
    before = shifted(x[:, -1:], "space", 1)
    after = shifted(x[:, :1], "space", -1)
    return jnp.concatenate([before, x, after], axis=1)


def shift_cols(value, steps):
    zero = jnp.zeros_like(value[:, :1])
    if steps == 1:
        return jnp.concatenate([zero, value[:, :-1]], axis=1)
    return jnp.concatenate([value[:, 1:], zero], axis=1)


def block_of(ref, a, b):
    return ref[a : a + 2, b : b + 2].reshape(512, -1)


def forward_kernel(ext_ref, w_ref, cot_ref, out_ref, grad_ref):
    sums = []
    for c in range(3):
        acc = jnp.zeros((512, 256), jnp.float32)
        for a in range(3):
            for b in range(3):
                acc += jnp.dot(
                    block_of(ext_ref, a, b), w_ref[a, b, c], preferred_element_type=jnp.float32
                )
        sums.append(acc.reshape(4, 128, 256))
    preact = shift_cols(sums[0], 1) + sums[1] + shift_cols(sums[2], -1)
    own = ext_ref[2:4, 1:3].reshape(4, 128, 256).astype(jnp.float32)
    sigma = 1.0 / (1.0 + jnp.exp(-preact))
    out_ref[...] = (own + preact * sigma).astype(jnp.bfloat16).reshape(2, 2, 128, 256)
    cot = cot_ref[...].reshape(4, 128, 256).astype(jnp.float32)
    grad = cot * sigma * (1.0 + preact * (1.0 - sigma))
    grad_ref[...] = grad.astype(jnp.bfloat16).reshape(2, 2, 128, 256)


def backward_kernel(ext_ref, w_ref, cot_ref, out_ref):
    sums = []
    for c in range(3):
        acc = jnp.zeros((512, 256), jnp.float32)
        for a in range(3):
            for b in range(3):
                acc += lax.dot_general(
                    block_of(ext_ref, 2 - a, 2 - b),
                    w_ref[a, b, c],
                    (((1,), (1,)), ((), ())),
                    preferred_element_type=jnp.float32,
                )
        sums.append(acc.reshape(4, 128, 256))
    total = shift_cols(sums[0], -1) + sums[1] + shift_cols(sums[2], 1)
    cot = cot_ref[...].reshape(4, 128, 256).astype(jnp.float32)
    out_ref[...] = (cot + total).astype(jnp.bfloat16).reshape(2, 2, 128, 256)


def weight_kernel(mine_ref, theirs_ref, grad_ref, grad2_ref, order_ref, out_ref):
    order = order_ref[...]
    flipped = []
    for steps in (-1, 0, 1):
        parts = []
        for ref in (grad_ref, grad2_ref):
            value = ref[...].reshape(4, 128, 256)
            if steps:
                value = shift_cols(value.astype(jnp.float32), steps).astype(jnp.bfloat16)
            turned = lax.dot_general(
                order,
                value.reshape(512, 256),
                (((1,), (1,)), ((), ())),
                preferred_element_type=jnp.float32,
            )
            parts.append(turned.astype(jnp.bfloat16))
        flipped.append(jnp.concatenate(parts, axis=1))
    for a in range(3):
        for b in range(3):
            cells = jnp.concatenate(
                [block_of(mine_ref, a, b), block_of(theirs_ref, a, b)], axis=0
            )
            for c in range(3):
                tap = (a * 3 + b) * 3 + c
                out_ref[:, tap * 128 : (tap + 1) * 128] = jnp.dot(
                    flipped[c], cells, preferred_element_type=jnp.float32
                ).astype(jnp.bfloat16)


def call(kernel, shapes, flops):
    return pl.pallas_call(
        kernel,
        out_shape=shapes,
        compiler_params=VMEM,
        cost_estimate=pl.CostEstimate(flops=flops, bytes_accessed=5000000, transcendentals=0),
    )


def row_order():
    channels = np.arange(256).reshape(2, 8, 8, 2).transpose(0, 2, 1, 3).reshape(256)
    return (channels[:, None] == np.arange(256)[None, :]).astype(np.float32)


def local(frames_in, weight, cotangent):
    core = lax.axis_index("tm") % 2
    block = jax.ShapeDtypeStruct((2, 2, 128, 256), jnp.bfloat16)
    flops = 2 * 512 * 6912 * 256

    carried = shifted(frames_in, "tm", 1)
    ext = with_rows(jnp.concatenate([carried, frames_in], axis=0))
    low, high = ext[..., :128], ext[..., 128:]
    mine = jnp.where(core == 0, low, high)
    theirs = flip_core(jnp.where(core == 0, high, low))
    output, grad_pre = call(forward_kernel, (block, block), flops)(ext, weight, cotangent)

    grad_other = flip_core(grad_pre)
    order = jnp.asarray(row_order(), jnp.bfloat16)
    terms = call(weight_kernel, jax.ShapeDtypeStruct((256, 3456), jnp.bfloat16), flops)(
        mine, theirs, grad_pre, grad_other, order
    )
    got = exchange(terms, ("x_lo", "x_hi", "y")).reshape(16, 16, 3456)
    plane = jnp.sum(got.astype(jnp.float32), axis=0)
    got = exchange(plane, ("z",)).reshape(8, 2, 3456)
    scale = 1.0 / math.sqrt(32.0 * 32.0 * 128.0)
    total = jnp.sum(got, axis=0) * jnp.float32(scale)
    share = lax.all_gather(total, "tm", axis=0, tiled=False)
    share = share.reshape(8, 2, 2, 27, 128).transpose(0, 2, 3, 1, 4)
    grad_weight = share.reshape(16, 3, 3, 3, 256)

    follow = shifted(grad_pre, "tm", -1)
    grad_ext = with_rows(jnp.concatenate([grad_pre, follow], axis=0))
    grad_input = call(backward_kernel, block, flops)(grad_ext, weight, cotangent)
    return (output, grad_input, grad_weight)


def solution(mesh):
    placed = (P("tm", "space", None, None), P(), P("tm", "space", None, None))
    return jax.shard_map(
        local,
        mesh=mesh,
        in_specs=placed,
        out_specs=(
            P("tm", "space", None, None),
            P("tm", "space", None, None),
            P("space", None, None, None, None),
        ),
        check_vma=False,
    )
```

```python
import functools
import itertools
import math

import jax
import jax.numpy as jnp
import numpy as np
from jax import lax
from jax.experimental import pallas as pl
from jax.experimental.pallas import tpu as pltpu
from jax.sharding import PartitionSpec as P

BOTH = ("tm", "space")
VMEM = pltpu.CompilerParams(vmem_limit_bytes=48 * 1024 * 1024)
SIZES = {"x_hi": 2, "y": 4, "core": 2, "x_lo": 2, "z": 8}


def groups_of(names):
    rest = [n for n in SIZES if n not in names]
    groups = []
    for fixed in itertools.product(*(range(SIZES[n]) for n in rest)):
        group = []
        for varied in itertools.product(*(range(SIZES[n]) for n in names)):
            at = dict(zip(rest, fixed)) | dict(zip(names, varied))
            tm = (at["x_hi"] * 4 + at["y"]) * 2 + at["core"]
            group.append(tm * 16 + at["x_lo"] * 8 + at["z"])
        groups.append(group)
    return groups


def exchange(value, names):
    return lax.all_to_all(value, BOTH, 0, 0, tiled=True, axis_index_groups=groups_of(names))


def flip_core(value):
    return lax.ppermute(value, "tm", [(i, i ^ 1) for i in range(16)])


def shifted(value, axis, steps):
    count = lax.axis_size(axis)
    leading, last = (max(0, -steps), min(count, count - steps))
    return lax.ppermute(value, axis, [(source, source + steps) for source in range(leading, last)])


def with_rows(first, second):
    before = shifted(jnp.concatenate([first[:, -1:], second[:, -1:]], axis=0), "space", 1)
    after = shifted(jnp.concatenate([first[:, :1], second[:, :1]], axis=0), "space", -1)
    return jnp.concatenate([before, jnp.concatenate([first, second], axis=0), after], axis=1)


def shift_cols(value, steps):
    zero = jnp.zeros_like(value[:, :1])
    if steps == 1:
        return jnp.concatenate([zero, value[:, :-1]], axis=1)
    return jnp.concatenate([value[:, 1:], zero], axis=1)


def block_of(ref, a, b):
    return ref[a : a + 2, b : b + 2].reshape(512, -1)


def forward_kernel(ext_ref, w_ref, cot_ref, out_ref, grad_ref):
    sums = []
    for c in range(3):
        acc = jnp.zeros((512, 256), jnp.float32)
        for a in range(3):
            for b in range(3):
                acc += jnp.dot(
                    block_of(ext_ref, a, b), w_ref[a, b, c], preferred_element_type=jnp.float32
                )
        sums.append(acc.reshape(4, 128, 256))
    preact = shift_cols(sums[0], 1) + sums[1] + shift_cols(sums[2], -1)
    own = ext_ref[2:4, 1:3].reshape(4, 128, 256).astype(jnp.float32)
    sigma = 1.0 / (1.0 + jnp.exp(-preact))
    out_ref[...] = (own + preact * sigma).astype(jnp.bfloat16).reshape(2, 2, 128, 256)
    cot = cot_ref[...].reshape(4, 128, 256).astype(jnp.float32)
    grad = cot * sigma * (1.0 + preact * (1.0 - sigma))
    grad_ref[...] = grad.astype(jnp.bfloat16).reshape(2, 2, 128, 256)


def backward_kernel(ext_ref, w_ref, cot_ref, out_ref):
    sums = []
    for c in range(3):
        acc = jnp.zeros((512, 256), jnp.float32)
        for a in range(3):
            for b in range(3):
                acc += lax.dot_general(
                    block_of(ext_ref, 2 - a, 2 - b),
                    w_ref[a, b, c],
                    (((1,), (1,)), ((), ())),
                    preferred_element_type=jnp.float32,
                )
        sums.append(acc.reshape(4, 128, 256))
    total = shift_cols(sums[0], -1) + sums[1] + shift_cols(sums[2], 1)
    cot = cot_ref[...].reshape(4, 128, 256).astype(jnp.float32)
    out_ref[...] = (cot + total).astype(jnp.bfloat16).reshape(2, 2, 128, 256)


def weight_kernel(mine_ref, theirs_ref, grad_ref, grad2_ref, order_ref, out_ref):
    order = order_ref[...]
    flipped = []
    for steps in (-1, 0, 1):
        parts = []
        for ref in (grad_ref, grad2_ref):
            value = ref[...].reshape(4, 128, 256)
            if steps:
                value = shift_cols(value.astype(jnp.float32), steps).astype(jnp.bfloat16)
            turned = lax.dot_general(
                order,
                value.reshape(512, 256),
                (((1,), (1,)), ((), ())),
                preferred_element_type=jnp.float32,
            )
            parts.append(turned.astype(jnp.bfloat16))
        flipped.append(jnp.concatenate(parts, axis=1))
    turned = jnp.concatenate(flipped, axis=0)
    taps = [(a, b) for a in range(3) for b in range(3)]
    for start in range(0, 9, 2):
        some = taps[start : start + 2]
        cells = jnp.concatenate(
            [
                jnp.concatenate([block_of(mine_ref, a, b) for a, b in some], axis=1),
                jnp.concatenate([block_of(theirs_ref, a, b) for a, b in some], axis=1),
            ],
            axis=0,
        )
        terms = jnp.dot(turned, cells, preferred_element_type=jnp.float32).astype(jnp.bfloat16)
        for i in range(len(some)):
            for c in range(3):
                tap = (start + i) * 3 + c
                out_ref[:, tap * 128 : (tap + 1) * 128] = terms[
                    c * 256 : (c + 1) * 256, i * 128 : (i + 1) * 128
                ]


def edge_kernel(first_ref, second_ref, last_ref, leading_ref):
    for i, ref in enumerate((first_ref, second_ref)):
        last_ref[2 * i : 2 * i + 2] = ref[:, 1:]
        leading_ref[2 * i : 2 * i + 2] = ref[:, :1]


def plane_kernel(got_ref, out_ref):
    total = got_ref[0].astype(jnp.float32)
    for i in range(1, 16):
        total += got_ref[i].astype(jnp.float32)
    for z in range(8):
        out_ref[z] = total[2 * z : 2 * z + 2].astype(out_ref.dtype)


def line_kernel(got_ref, out_ref):
    total = got_ref[0].astype(jnp.float32)
    for i in range(1, 8):
        total += got_ref[i].astype(jnp.float32)
    total *= 1.0 / math.sqrt(32.0 * 32.0 * 128.0)
    for i in range(8):
        out_ref[i] = total


def share_kernel(mine_ref, other_ref, out_ref):
    core = lax.axis_index("tm") % 2
    for tap in range(27):
        lanes = slice(tap * 128, (tap + 1) * 128)
        mine = jnp.concatenate([mine_ref[q, :, lanes] for q in range(8)], axis=0)
        other = jnp.concatenate([other_ref[q, :, lanes] for q in range(8)], axis=0)
        out_ref[tap] = jnp.where(
            core == 0,
            jnp.concatenate([mine, other], axis=1),
            jnp.concatenate([other, mine], axis=1),
        )


def call(kernel, shapes, flops):
    return pl.pallas_call(
        kernel,
        out_shape=shapes,
        compiler_params=VMEM,
        cost_estimate=pl.CostEstimate(flops=flops, bytes_accessed=5000000, transcendentals=0),
    )


def row_order():
    channels = np.arange(256).reshape(2, 8, 8, 2).transpose(0, 2, 1, 3).reshape(256)
    return (channels[:, None] == np.arange(256)[None, :]).astype(np.float32)


def local(frames_in, weight, cotangent):
    core = lax.axis_index("tm") % 2
    block = jax.ShapeDtypeStruct((2, 2, 128, 256), jnp.bfloat16)
    flops = 2 * 512 * 6912 * 256

    carried = shifted(frames_in, "tm", 1)
    ext = with_rows(carried, frames_in)
    low, high = ext[..., :128], ext[..., 128:]
    mine = jnp.where(core == 0, low, high)
    theirs = flip_core(jnp.where(core == 0, high, low))
    output, grad_pre = call(forward_kernel, (block, block), flops)(ext, weight, cotangent)

    grad_other = flip_core(grad_pre)
    order = jnp.asarray(row_order(), jnp.bfloat16)
    terms = call(weight_kernel, jax.ShapeDtypeStruct((256, 3456), jnp.bfloat16), flops)(
        mine, theirs, grad_pre, grad_other, order
    )
    follow = shifted(grad_pre, "tm", -1)
    got = exchange(terms, ("x_lo", "x_hi", "y")).reshape(16, 16, 3456)
    plane = pl.pallas_call(
        plane_kernel,
        out_shape=jax.ShapeDtypeStruct((8, 2, 3456), jnp.bfloat16),
        grid=(3,),
        in_specs=[pl.BlockSpec((16, 16, 1152), lambda i: (0, 0, i))],
        out_specs=pl.BlockSpec((8, 2, 1152), lambda i: (0, 0, i)),
        compiler_params=VMEM,
    )(got)
    held, follow, plane = lax.optimization_barrier((grad_pre, follow, plane))
    edge = jax.ShapeDtypeStruct((4, 1, 128, 256), jnp.bfloat16)
    last, leading = call(edge_kernel, (edge, edge), flops)(held, follow)
    got = exchange(plane, ("z",)).reshape(8, 2, 3456)
    got, _, _ = lax.optimization_barrier((got, last, leading))
    before = shifted(last, "space", 1)
    after = shifted(leading, "space", -1)
    grad_ext = jnp.concatenate([before, jnp.concatenate([held, follow], axis=0), after], axis=1)
    copies = call(line_kernel, jax.ShapeDtypeStruct((8, 2, 3456), jnp.float32), 100000)(got)
    copies, grad_ext = lax.optimization_barrier((copies, grad_ext))
    share = exchange(copies, ("x_hi", "y")).reshape(8, 2, 3456)
    grad_input = call(backward_kernel, block, flops)(grad_ext, weight, cotangent)
    share, grad_input = lax.optimization_barrier((share, grad_input))
    other = flip_core(share)
    share = call(share_kernel, jax.ShapeDtypeStruct((27, 16, 256), jnp.float32), 100000)(
        share, other
    )
    grad_weight = share.transpose(1, 0, 2).reshape(16, 3, 3, 3, 256)
    return (output, grad_input, grad_weight)


def solution(mesh):
    placed = (P("tm", "space", None, None), P(), P("tm", "space", None, None))
    return jax.shard_map(
        local,
        mesh=mesh,
        in_specs=placed,
        out_specs=(
            P("tm", "space", None, None),
            P("tm", "space", None, None),
            P("space", None, None, None, None),
        ),
        check_vma=False,
    )
```

```python
import functools
import itertools
import math

import jax
import jax.numpy as jnp
import numpy as np
from jax import lax
from jax.experimental import pallas as pl
from jax.experimental.pallas import tpu as pltpu
from jax.sharding import PartitionSpec as P

BOTH = ("tm", "space")
VMEM = pltpu.CompilerParams(vmem_limit_bytes=20 * 1024 * 1024)
SIZES = {"x_hi": 2, "y": 4, "core": 2, "x_lo": 2, "z": 8}


def groups_of(names):
    rest = [n for n in SIZES if n not in names]
    groups = []
    for fixed in itertools.product(*(range(SIZES[n]) for n in rest)):
        group = []
        for varied in itertools.product(*(range(SIZES[n]) for n in names)):
            at = dict(zip(rest, fixed)) | dict(zip(names, varied))
            tm = (at["x_hi"] * 4 + at["y"]) * 2 + at["core"]
            group.append(tm * 16 + at["x_lo"] * 8 + at["z"])
        groups.append(group)
    return groups


def exchange(value, names):
    return lax.all_to_all(value, BOTH, 0, 0, tiled=True, axis_index_groups=groups_of(names))


def flip_core(value):
    return lax.ppermute(value, "tm", [(i, i ^ 1) for i in range(16)])


def shifted(value, axis, steps):
    count = lax.axis_size(axis)
    leading, last = (max(0, -steps), min(count, count - steps))
    return lax.ppermute(value, axis, [(source, source + steps) for source in range(leading, last)])


def shift_cols(value, steps):
    zero = jnp.zeros_like(value[:, :1])
    if steps == 1:
        return jnp.concatenate([zero, value[:, :-1]], axis=1)
    return jnp.concatenate([value[:, 1:], zero], axis=1)


def block_of(ref, a, b):
    return ref[a : a + 2, b : b + 2].reshape(512, -1)


def near_kernel(carried_ref, own_ref, w_ref, part_ref):
    sums = []
    for c in range(3):
        both = jnp.zeros((512, 256), jnp.float32)
        upper = jnp.zeros((256, 256), jnp.float32)
        lower = jnp.zeros((256, 256), jnp.float32)
        for a in range(3):
            if a == 0:
                block = carried_ref[...]
            elif a == 1:
                block = jnp.concatenate([carried_ref[1:], own_ref[:1]], axis=0)
            else:
                block = own_ref[...]
            rows = [block[:, r].reshape(256, 256) for r in range(2)]
            both += jnp.dot(
                jnp.concatenate(rows, axis=0), w_ref[a, 1, c], preferred_element_type=jnp.float32
            )
            upper += jnp.dot(rows[1], w_ref[a, 2, c], preferred_element_type=jnp.float32)
            lower += jnp.dot(rows[0], w_ref[a, 0, c], preferred_element_type=jnp.float32)
        sums.append((both + jnp.concatenate([upper, lower], axis=0)).reshape(4, 128, 256))
    part_ref[...] = shift_cols(sums[0], 1) + sums[1] + shift_cols(sums[2], -1)


def forward_kernel(before_ref, after_ref, own_ref, part_ref, w_ref, cot_ref, out_ref, grad_ref):
    sums = []
    for c in range(3):
        upper = jnp.zeros((256, 256), jnp.float32)
        lower = jnp.zeros((256, 256), jnp.float32)
        for a in range(3):
            top = before_ref[a : a + 2].reshape(256, 256)
            bottom = after_ref[a : a + 2].reshape(256, 256)
            upper += jnp.dot(top, w_ref[a, 0, c], preferred_element_type=jnp.float32)
            lower += jnp.dot(bottom, w_ref[a, 2, c], preferred_element_type=jnp.float32)
        sums.append(jnp.concatenate([upper, lower], axis=0).reshape(4, 128, 256))
    total = part_ref[...] + shift_cols(sums[0], 1) + sums[1] + shift_cols(sums[2], -1)
    for row in range(2):
        preact = total[2 * row : 2 * row + 2]
        own = own_ref[:, row].astype(jnp.float32)
        sigma = 1.0 / (1.0 + jnp.exp(-preact))
        out_ref[:, row] = (own + preact * sigma).astype(jnp.bfloat16)
        cot = cot_ref[:, row].astype(jnp.float32)
        grad = cot * sigma * (1.0 + preact * (1.0 - sigma))
        grad_ref[:, row] = grad.astype(jnp.bfloat16)


def backward_kernel(ext_ref, w_ref, cot_ref, out_ref):
    sums = []
    for c in range(3):
        acc = jnp.zeros((512, 256), jnp.float32)
        for a in range(3):
            for b in range(3):
                acc += lax.dot_general(
                    block_of(ext_ref, 2 - a, 2 - b),
                    w_ref[a, b, c],
                    (((1,), (1,)), ((), ())),
                    preferred_element_type=jnp.float32,
                )
        sums.append(acc.reshape(4, 128, 256))
    total = shift_cols(sums[0], -1) + sums[1] + shift_cols(sums[2], 1)
    cot = cot_ref[...].reshape(4, 128, 256).astype(jnp.float32)
    out_ref[...] = (cot + total).astype(jnp.bfloat16).reshape(2, 2, 128, 256)


def turned_grad(grad_ref, order_ref):
    parts = []
    for steps in (-1, 0, 1):
        value = grad_ref[...].reshape(4, 128, 256)
        if steps:
            value = shift_cols(value.astype(jnp.float32), steps).astype(jnp.bfloat16)
        turned = lax.dot_general(
            order_ref[...],
            value.reshape(512, 256),
            (((1,), (1,)), ((), ())),
            preferred_element_type=jnp.float32,
        )
        parts.append(turned.astype(jnp.bfloat16))
    return jnp.concatenate(parts, axis=0)


TAPS = [(a, b) for a in range(3) for b in range(3)]


def own_terms_kernel(cells_ref, grad_ref, order_ref, out_ref):
    turned = turned_grad(grad_ref, order_ref)
    for start in range(0, 9, 2):
        some = TAPS[start : start + 2]
        cells = jnp.concatenate([block_of(cells_ref, a, b) for a, b in some], axis=1)
        out_ref[:, start * 128 : (start + len(some)) * 128] = jnp.dot(
            turned, cells, preferred_element_type=jnp.float32
        )


def terms_kernel(cells_ref, grad_ref, order_ref, part_ref, out_ref):
    turned = turned_grad(grad_ref, order_ref)
    for start in range(0, 9, 2):
        some = TAPS[start : start + 2]
        cells = jnp.concatenate([block_of(cells_ref, a, b) for a, b in some], axis=1)
        terms = jnp.dot(turned, cells, preferred_element_type=jnp.float32)
        terms += part_ref[:, start * 128 : (start + len(some)) * 128]
        terms = terms.astype(jnp.bfloat16)
        for i in range(len(some)):
            for c in range(3):
                tap = (start + i) * 3 + c
                out_ref[:, tap * 128 : (tap + 1) * 128] = terms[
                    c * 256 : (c + 1) * 256, i * 128 : (i + 1) * 128
                ]


def plane_kernel(got_ref, out_ref):
    total = got_ref[0].astype(jnp.float32)
    for i in range(1, 16):
        total += got_ref[i].astype(jnp.float32)
    for z in range(8):
        out_ref[z] = total[2 * z : 2 * z + 2].astype(out_ref.dtype)


def line_kernel(got_ref, out_ref):
    total = got_ref[0].astype(jnp.float32)
    for i in range(1, 8):
        total += got_ref[i].astype(jnp.float32)
    total *= 1.0 / math.sqrt(32.0 * 32.0 * 128.0)
    for i in range(8):
        out_ref[i] = total


def share_kernel(mine_ref, other_ref, out_ref):
    core = lax.axis_index("tm") % 2
    for tap in range(27):
        lanes = slice(tap * 128, (tap + 1) * 128)
        mine = jnp.concatenate([mine_ref[q, :, lanes] for q in range(8)], axis=0)
        other = jnp.concatenate([other_ref[q, :, lanes] for q in range(8)], axis=0)
        out_ref[tap] = jnp.where(
            core == 0,
            jnp.concatenate([mine, other], axis=1),
            jnp.concatenate([other, mine], axis=1),
        )


def call(kernel, shapes, flops):
    return pl.pallas_call(
        kernel,
        out_shape=shapes,
        compiler_params=VMEM,
        cost_estimate=pl.CostEstimate(flops=flops, bytes_accessed=5000000, transcendentals=0),
    )


def row_order():
    channels = np.arange(256).reshape(2, 8, 8, 2).transpose(0, 2, 1, 3).reshape(256)
    return (channels[:, None] == np.arange(256)[None, :]).astype(np.float32)


def local(frames_in, weight, cotangent):
    core = lax.axis_index("tm") % 2
    block = jax.ShapeDtypeStruct((2, 2, 128, 256), jnp.bfloat16)
    flops = 2 * 512 * 6912 * 256

    carried = shifted(frames_in, "tm", 1)
    before = shifted(jnp.concatenate([carried[:, 1:], frames_in[:, 1:]], axis=0), "space", 1)
    after = shifted(jnp.concatenate([carried[:, :1], frames_in[:, :1]], axis=0), "space", -1)
    part = jax.ShapeDtypeStruct((4, 128, 256), jnp.float32)
    part = call(near_kernel, part, flops)(carried, frames_in, weight)
    before, after, part = lax.optimization_barrier((before, after, part))
    ext = jnp.concatenate(
        [before, jnp.concatenate([carried, frames_in], axis=0), after], axis=1
    )
    low, high = ext[..., :128], ext[..., 128:]
    mine = jnp.where(core == 0, low, high)
    theirs = flip_core(jnp.where(core == 0, high, low))
    output, grad_pre = call(forward_kernel, (block, block), flops // 3)(
        before, after, frames_in, part, weight, cotangent
    )
    grad_other = flip_core(grad_pre)
    order = jnp.asarray(row_order(), jnp.bfloat16)
    own_terms = call(own_terms_kernel, jax.ShapeDtypeStruct((768, 1152), jnp.float32), flops // 2)(
        mine, grad_pre, order
    )
    terms = call(terms_kernel, jax.ShapeDtypeStruct((256, 3456), jnp.bfloat16), flops // 2)(
        theirs, grad_other, order, own_terms
    )
    above = shifted(grad_pre[:, 1:], "space", 1)
    below = shifted(grad_pre[:, :1], "space", -1)
    tall = jnp.concatenate([above, grad_pre, below], axis=1)
    follow = shifted(tall, "tm", -1)
    got = exchange(terms, ("x_lo", "x_hi", "y")).reshape(16, 16, 3456)
    plane = pl.pallas_call(
        plane_kernel,
        out_shape=jax.ShapeDtypeStruct((8, 2, 3456), jnp.bfloat16),
        grid=(3,),
        in_specs=[pl.BlockSpec((16, 16, 1152), lambda i: (0, 0, i))],
        out_specs=pl.BlockSpec((8, 2, 1152), lambda i: (0, 0, i)),
        compiler_params=VMEM,
    )(got)
    got = exchange(plane, ("z",)).reshape(8, 2, 3456)
    copies = call(line_kernel, jax.ShapeDtypeStruct((8, 2, 3456), jnp.float32), 100000)(got)
    copies, tall, follow = lax.optimization_barrier((copies, tall, follow))
    grad_ext = jnp.concatenate([tall, follow], axis=0)
    share = exchange(copies, ("x_hi", "y")).reshape(8, 2, 3456)
    grad_input = call(backward_kernel, block, flops)(grad_ext, weight, cotangent)
    share, grad_input = lax.optimization_barrier((share, grad_input))
    other = flip_core(share)
    share = call(share_kernel, jax.ShapeDtypeStruct((27, 16, 256), jnp.float32), 100000)(
        share, other
    )
    grad_weight = share.transpose(1, 0, 2).reshape(16, 3, 3, 3, 256)
    return (output, grad_input, grad_weight)


def solution(mesh):
    placed = (P("tm", "space", None, None), P(), P("tm", "space", None, None))
    return jax.shard_map(
        local,
        mesh=mesh,
        in_specs=placed,
        out_specs=(
            P("tm", "space", None, None),
            P("tm", "space", None, None),
            P("space", None, None, None, None),
        ),
        check_vma=False,
    )
```

```python
import functools
import itertools
import math

import jax
import jax.numpy as jnp
import numpy as np
from jax import lax
from jax.experimental import pallas as pl
from jax.experimental.pallas import tpu as pltpu
from jax.sharding import PartitionSpec as P

BOTH = ("tm", "space")
VMEM = pltpu.CompilerParams(vmem_limit_bytes=20 * 1024 * 1024)
SIZES = {"x_hi": 2, "y": 4, "core": 2, "x_lo": 2, "z": 8}


def groups_of(names):
    rest = [n for n in SIZES if n not in names]
    groups = []
    for fixed in itertools.product(*(range(SIZES[n]) for n in rest)):
        group = []
        for varied in itertools.product(*(range(SIZES[n]) for n in names)):
            at = dict(zip(rest, fixed)) | dict(zip(names, varied))
            tm = (at["x_hi"] * 4 + at["y"]) * 2 + at["core"]
            group.append(tm * 16 + at["x_lo"] * 8 + at["z"])
        groups.append(group)
    return groups


def exchange(value, names):
    return lax.all_to_all(value, BOTH, 0, 0, tiled=True, axis_index_groups=groups_of(names))


def flip_core(value):
    return lax.ppermute(value, "tm", [(i, i ^ 1) for i in range(16)])


def shifted(value, axis, steps):
    count = lax.axis_size(axis)
    leading, last = (max(0, -steps), min(count, count - steps))
    return lax.ppermute(value, axis, [(source, source + steps) for source in range(leading, last)])


def pairs(value, first):
    links = [(i, i + 1) for i in range(first, 15, 2)]
    return lax.ppermute(value, "space", links + [(j, i) for i, j in links])


def row_halo(top, bottom):
    even = lax.axis_index("space") % 2 == 0
    near = pairs(jnp.where(even, bottom, top), 0)
    far = pairs(jnp.where(even, top, bottom), 1)
    return near, far


def shift_cols(value, steps):
    zero = jnp.zeros_like(value[:, :1])
    if steps == 1:
        return jnp.concatenate([zero, value[:, :-1]], axis=1)
    return jnp.concatenate([value[:, 1:], zero], axis=1)


def block_of(ref, a, b):
    return ref[a : a + 2, b : b + 2].reshape(512, -1)


def near_kernel(carried_ref, own_ref, w_ref, part_ref):
    sums = []
    for c in range(3):
        both = jnp.zeros((512, 256), jnp.float32)
        upper = jnp.zeros((256, 256), jnp.float32)
        lower = jnp.zeros((256, 256), jnp.float32)
        for a in range(3):
            if a == 0:
                block = carried_ref[...]
            elif a == 1:
                block = jnp.concatenate([carried_ref[1:], own_ref[:1]], axis=0)
            else:
                block = own_ref[...]
            rows = [block[:, r].reshape(256, 256) for r in range(2)]
            both += jnp.dot(
                jnp.concatenate(rows, axis=0), w_ref[a, 1, c], preferred_element_type=jnp.float32
            )
            upper += jnp.dot(rows[1], w_ref[a, 2, c], preferred_element_type=jnp.float32)
            lower += jnp.dot(rows[0], w_ref[a, 0, c], preferred_element_type=jnp.float32)
        sums.append((both + jnp.concatenate([upper, lower], axis=0)).reshape(4, 128, 256))
    part_ref[...] = shift_cols(sums[0], 1) + sums[1] + shift_cols(sums[2], -1)


def forward_kernel(before_ref, after_ref, own_ref, part_ref, w_ref, cot_ref, out_ref, grad_ref):
    sums = []
    for c in range(3):
        upper = jnp.zeros((256, 256), jnp.float32)
        lower = jnp.zeros((256, 256), jnp.float32)
        for a in range(3):
            top = before_ref[a : a + 2].reshape(256, 256)
            bottom = after_ref[a : a + 2].reshape(256, 256)
            upper += jnp.dot(top, w_ref[a, 0, c], preferred_element_type=jnp.float32)
            lower += jnp.dot(bottom, w_ref[a, 2, c], preferred_element_type=jnp.float32)
        sums.append(jnp.concatenate([upper, lower], axis=0).reshape(4, 128, 256))
    total = part_ref[...] + shift_cols(sums[0], 1) + sums[1] + shift_cols(sums[2], -1)
    for row in range(2):
        preact = total[2 * row : 2 * row + 2]
        own = own_ref[:, row].astype(jnp.float32)
        sigma = 1.0 / (1.0 + jnp.exp(-preact))
        out_ref[:, row] = (own + preact * sigma).astype(jnp.bfloat16)
        cot = cot_ref[:, row].astype(jnp.float32)
        grad = cot * sigma * (1.0 + preact * (1.0 - sigma))
        grad_ref[:, row] = grad.astype(jnp.bfloat16)


def backward_kernel(ext_ref, w_ref, cot_ref, out_ref):
    sums = []
    for c in range(3):
        acc = jnp.zeros((512, 256), jnp.float32)
        for a in range(3):
            for b in range(3):
                acc += lax.dot_general(
                    block_of(ext_ref, 2 - a, 2 - b),
                    w_ref[a, b, c],
                    (((1,), (1,)), ((), ())),
                    preferred_element_type=jnp.float32,
                )
        sums.append(acc.reshape(4, 128, 256))
    total = shift_cols(sums[0], -1) + sums[1] + shift_cols(sums[2], 1)
    cot = cot_ref[...].reshape(4, 128, 256).astype(jnp.float32)
    out_ref[...] = (cot + total).astype(jnp.bfloat16).reshape(2, 2, 128, 256)


def turned_grad(grad_ref, order_ref):
    parts = []
    for steps in (-1, 0, 1):
        value = grad_ref[...].reshape(4, 128, 256)
        if steps:
            value = shift_cols(value.astype(jnp.float32), steps).astype(jnp.bfloat16)
        turned = lax.dot_general(
            order_ref[...],
            value.reshape(512, 256),
            (((1,), (1,)), ((), ())),
            preferred_element_type=jnp.float32,
        )
        parts.append(turned.astype(jnp.bfloat16))
    return jnp.concatenate(parts, axis=0)


TAPS = [(a, b) for a in range(3) for b in range(3)]


def own_terms_kernel(cells_ref, grad_ref, order_ref, out_ref):
    turned = turned_grad(grad_ref, order_ref)
    for start in range(0, 9, 2):
        some = TAPS[start : start + 2]
        cells = jnp.concatenate([block_of(cells_ref, a, b) for a, b in some], axis=1)
        out_ref[:, start * 128 : (start + len(some)) * 128] = jnp.dot(
            turned, cells, preferred_element_type=jnp.float32
        )


def terms_kernel(cells_ref, grad_ref, order_ref, part_ref, out_ref, held_ref, sems):
    turned = turned_grad(grad_ref, order_ref)
    copies = []
    for start in range(0, 9, 2):
        some = TAPS[start : start + 2]
        cells = jnp.concatenate([block_of(cells_ref, a, b) for a, b in some], axis=1)
        terms = jnp.dot(turned, cells, preferred_element_type=jnp.float32)
        terms += part_ref[:, start * 128 : (start + len(some)) * 128]
        terms = terms.astype(jnp.bfloat16)
        for i in range(len(some)):
            for c in range(3):
                tap = (start + i) * 3 + c
                held_ref[:, tap * 128 : (tap + 1) * 128] = terms[
                    c * 256 : (c + 1) * 256, i * 128 : (i + 1) * 128
                ]
        lanes = pl.ds(start * 384, len(some) * 384)
        copy = pltpu.make_async_copy(
            held_ref.at[:, lanes], out_ref.at[:, lanes], sems.at[start // 2]
        )
        copy.start()
        copies.append(copy)
    for copy in copies:
        copy.wait()


def plane_kernel(got_ref, out_ref):
    total = got_ref[0].astype(jnp.float32)
    for i in range(1, 16):
        total += got_ref[i].astype(jnp.float32)
    for z in range(8):
        out_ref[z] = total[2 * z : 2 * z + 2].astype(out_ref.dtype)


def line_kernel(got_ref, out_ref):
    total = got_ref[0].astype(jnp.float32)
    for i in range(1, 8):
        total += got_ref[i].astype(jnp.float32)
    total *= 1.0 / math.sqrt(32.0 * 32.0 * 128.0)
    for i in range(8):
        out_ref[i] = total


def share_kernel(mine_ref, other_ref, out_ref):
    core = lax.axis_index("tm") % 2
    for tap in range(27):
        lanes = slice(tap * 128, (tap + 1) * 128)
        mine = jnp.concatenate([mine_ref[q, :, lanes] for q in range(8)], axis=0)
        other = jnp.concatenate([other_ref[q, :, lanes] for q in range(8)], axis=0)
        out_ref[tap] = jnp.where(
            core == 0,
            jnp.concatenate([mine, other], axis=1),
            jnp.concatenate([other, mine], axis=1),
        )


def call(kernel, shapes, flops):
    return pl.pallas_call(
        kernel,
        out_shape=shapes,
        compiler_params=VMEM,
        cost_estimate=pl.CostEstimate(flops=flops, bytes_accessed=5000000, transcendentals=0),
    )


def row_order():
    channels = np.arange(256).reshape(2, 8, 8, 2).transpose(0, 2, 1, 3).reshape(256)
    return (channels[:, None] == np.arange(256)[None, :]).astype(np.float32)


def local(frames_in, weight, cotangent):
    core = lax.axis_index("tm") % 2
    block = jax.ShapeDtypeStruct((2, 2, 128, 256), jnp.bfloat16)
    flops = 2 * 512 * 6912 * 256

    carried = shifted(frames_in, "tm", 1)
    even = lax.axis_index("space") % 2 == 0
    near, far = row_halo(
        jnp.concatenate([carried[:, :1], frames_in[:, :1]], axis=0),
        jnp.concatenate([carried[:, 1:], frames_in[:, 1:]], axis=0),
    )
    part = jax.ShapeDtypeStruct((4, 128, 256), jnp.float32)
    part = call(near_kernel, part, flops)(carried, frames_in, weight)
    near, far, part = lax.optimization_barrier((near, far, part))
    before, after = jnp.where(even, far, near), jnp.where(even, near, far)
    ext = jnp.concatenate(
        [before, jnp.concatenate([carried, frames_in], axis=0), after], axis=1
    )
    low, high = ext[..., :128], ext[..., 128:]
    mine = jnp.where(core == 0, low, high)
    theirs = flip_core(jnp.where(core == 0, high, low))
    output, grad_pre = call(forward_kernel, (block, block), flops // 3)(
        before, after, frames_in, part, weight, cotangent
    )
    grad_other = flip_core(grad_pre)
    order = jnp.asarray(row_order(), jnp.bfloat16)
    own_terms = call(own_terms_kernel, jax.ShapeDtypeStruct((768, 1152), jnp.float32), flops // 2)(
        mine, grad_pre, order
    )
    terms = pl.pallas_call(
        terms_kernel,
        out_shape=jax.ShapeDtypeStruct((256, 3456), jnp.bfloat16),
        out_specs=pl.BlockSpec(memory_space=pl.ANY),
        scratch_shapes=[pltpu.VMEM((256, 3456), jnp.bfloat16), pltpu.SemaphoreType.DMA((5,))],
        compiler_params=VMEM,
        cost_estimate=pl.CostEstimate(flops=flops // 2, bytes_accessed=5000000, transcendentals=0),
    )(theirs, grad_other, order, own_terms)
    near, far = row_halo(grad_pre[:, :1], grad_pre[:, 1:])
    above, below = jnp.where(even, far, near), jnp.where(even, near, far)
    tall = jnp.concatenate([above, grad_pre, below], axis=1)
    follow = shifted(tall, "tm", -1)
    got = exchange(terms, ("x_lo", "x_hi", "y")).reshape(16, 16, 3456)
    plane = pl.pallas_call(
        plane_kernel,
        out_shape=jax.ShapeDtypeStruct((8, 2, 3456), jnp.bfloat16),
        grid=(3,),
        in_specs=[pl.BlockSpec((16, 16, 1152), lambda i: (0, 0, i))],
        out_specs=pl.BlockSpec((8, 2, 1152), lambda i: (0, 0, i)),
        compiler_params=VMEM,
    )(got)
    got = exchange(plane, ("z",)).reshape(8, 2, 3456)
    copies = call(line_kernel, jax.ShapeDtypeStruct((8, 2, 3456), jnp.float32), 100000)(got)
    copies, tall, follow = lax.optimization_barrier((copies, tall, follow))
    grad_ext = jnp.concatenate([tall, follow], axis=0)
    share = exchange(copies, ("x_hi", "y")).reshape(8, 2, 3456)
    grad_input = call(backward_kernel, block, flops)(grad_ext, weight, cotangent)
    share, grad_input = lax.optimization_barrier((share, grad_input))
    other = flip_core(share)
    share = call(share_kernel, jax.ShapeDtypeStruct((27, 16, 256), jnp.float32), 100000)(
        share, other
    )
    grad_weight = share.transpose(1, 0, 2).reshape(16, 3, 3, 3, 256)
    return (output, grad_input, grad_weight)


def solution(mesh):
    placed = (P("tm", "space", None, None), P(), P("tm", "space", None, None))
    return jax.shard_map(
        local,
        mesh=mesh,
        in_specs=placed,
        out_specs=(
            P("tm", "space", None, None),
            P("tm", "space", None, None),
            P("space", None, None, None, None),
        ),
        check_vma=False,
    )
```

```python
import functools
import itertools
import math

import jax
import jax.numpy as jnp
import numpy as np
from jax import lax
from jax.experimental import pallas as pl
from jax.experimental.pallas import tpu as pltpu
from jax.sharding import PartitionSpec as P

BOTH = ("tm", "space")
VMEM = pltpu.CompilerParams(vmem_limit_bytes=20 * 1024 * 1024)
SIZES = {"x_hi": 2, "y": 4, "core": 2, "x_lo": 2, "z": 8}


def groups_of(names):
    rest = [n for n in SIZES if n not in names]
    groups = []
    for fixed in itertools.product(*(range(SIZES[n]) for n in rest)):
        group = []
        for varied in itertools.product(*(range(SIZES[n]) for n in names)):
            at = dict(zip(rest, fixed)) | dict(zip(names, varied))
            tm = (at["x_hi"] * 4 + at["y"]) * 2 + at["core"]
            group.append(tm * 16 + at["x_lo"] * 8 + at["z"])
        groups.append(group)
    return groups


def exchange(value, names):
    return lax.all_to_all(value, BOTH, 0, 0, tiled=True, axis_index_groups=groups_of(names))


def flip_core(value):
    return lax.ppermute(value, "tm", [(i, i ^ 1) for i in range(16)])


def shifted(value, axis, steps):
    count = lax.axis_size(axis)
    leading, last = (max(0, -steps), min(count, count - steps))
    return lax.ppermute(value, axis, [(source, source + steps) for source in range(leading, last)])


def pairs(value, first):
    links = [(i, i + 1) for i in range(first, 15, 2)]
    return lax.ppermute(value, "space", links + [(j, i) for i, j in links])


def row_halo(top, bottom):
    even = lax.axis_index("space") % 2 == 0
    near = pairs(jnp.where(even, bottom, top), 0)
    far = pairs(jnp.where(even, top, bottom), 1)
    return near, far


def shift_cols(value, steps):
    zero = jnp.zeros_like(value[:, :1])
    if steps == 1:
        return jnp.concatenate([zero, value[:, :-1]], axis=1)
    return jnp.concatenate([value[:, 1:], zero], axis=1)


def block_of(ref, a, b):
    return ref[a : a + 2, b : b + 2].reshape(512, -1)


def edge_kernel(frames_ref, top_ref, bottom_ref, own_ref):
    top_ref[...] = frames_ref[:, :1]
    bottom_ref[...] = frames_ref[:, 1:]
    own_ref[...] = frames_ref[...]


def near_kernel(carried_ref, own_ref, w_from, part_ref, w_ref, sems):
    copies = [
        pltpu.make_async_copy(w_from.at[:, :, c], w_ref.at[:, :, c], sems.at[c]) for c in range(3)
    ]
    for copy in copies:
        copy.start()
    blocks = [
        carried_ref[...],
        jnp.concatenate([carried_ref[1:], own_ref[:1]], axis=0),
        own_ref[...],
    ]
    sums = []
    for c in range(3):
        both = jnp.zeros((512, 256), jnp.float32)
        upper = jnp.zeros((256, 256), jnp.float32)
        lower = jnp.zeros((256, 256), jnp.float32)
        copies[c].wait()
        for a in range(3):
            rows = [blocks[a][:, r].reshape(256, 256) for r in range(2)]
            both += jnp.dot(
                jnp.concatenate(rows, axis=0), w_ref[a, 1, c], preferred_element_type=jnp.float32
            )
            upper += jnp.dot(rows[1], w_ref[a, 2, c], preferred_element_type=jnp.float32)
            lower += jnp.dot(rows[0], w_ref[a, 0, c], preferred_element_type=jnp.float32)
        sums.append((both + jnp.concatenate([upper, lower], axis=0)).reshape(4, 128, 256))
    part_ref[...] = shift_cols(sums[0], 1) + sums[1] + shift_cols(sums[2], -1)


def forward_kernel(before_ref, after_ref, own_ref, part_ref, w_ref, cot_ref, out_ref, grad_ref):
    sums = []
    for c in range(3):
        upper = jnp.zeros((256, 256), jnp.float32)
        lower = jnp.zeros((256, 256), jnp.float32)
        for a in range(3):
            top = before_ref[a : a + 2].reshape(256, 256)
            bottom = after_ref[a : a + 2].reshape(256, 256)
            upper += jnp.dot(top, w_ref[a, 0, c], preferred_element_type=jnp.float32)
            lower += jnp.dot(bottom, w_ref[a, 2, c], preferred_element_type=jnp.float32)
        sums.append(jnp.concatenate([upper, lower], axis=0).reshape(4, 128, 256))
    total = part_ref[...] + shift_cols(sums[0], 1) + sums[1] + shift_cols(sums[2], -1)
    for row in range(2):
        preact = total[2 * row : 2 * row + 2]
        own = own_ref[:, row].astype(jnp.float32)
        sigma = 1.0 / (1.0 + jnp.exp(-preact))
        out_ref[:, row] = (own + preact * sigma).astype(jnp.bfloat16)
        cot = cot_ref[:, row].astype(jnp.float32)
        grad = cot * sigma * (1.0 + preact * (1.0 - sigma))
        grad_ref[:, row] = grad.astype(jnp.bfloat16)


def backward_kernel(ext_ref, w_ref, cot_ref, out_ref):
    sums = []
    for c in range(3):
        acc = jnp.zeros((512, 256), jnp.float32)
        for a in range(3):
            for b in range(3):
                acc += lax.dot_general(
                    block_of(ext_ref, 2 - a, 2 - b),
                    w_ref[a, b, c],
                    (((1,), (1,)), ((), ())),
                    preferred_element_type=jnp.float32,
                )
        sums.append(acc.reshape(4, 128, 256))
    total = shift_cols(sums[0], -1) + sums[1] + shift_cols(sums[2], 1)
    cot = cot_ref[...].reshape(4, 128, 256).astype(jnp.float32)
    out_ref[...] = (cot + total).astype(jnp.bfloat16).reshape(2, 2, 128, 256)


def turned_grad(grad_ref, order_ref):
    parts = []
    for steps in (-1, 0, 1):
        value = grad_ref[...].reshape(4, 128, 256)
        if steps:
            value = shift_cols(value.astype(jnp.float32), steps).astype(jnp.bfloat16)
        turned = lax.dot_general(
            order_ref[...],
            value.reshape(512, 256),
            (((1,), (1,)), ((), ())),
            preferred_element_type=jnp.float32,
        )
        parts.append(turned.astype(jnp.bfloat16))
    return jnp.concatenate(parts, axis=0)


TAPS = [(a, b) for a in range(3) for b in range(3)]


def own_terms_kernel(cells_ref, grad_ref, order_ref, out_ref):
    turned = turned_grad(grad_ref, order_ref)
    for start in range(0, 9, 2):
        some = TAPS[start : start + 2]
        cells = jnp.concatenate([block_of(cells_ref, a, b) for a, b in some], axis=1)
        out_ref[:, start * 128 : (start + len(some)) * 128] = jnp.dot(
            turned, cells, preferred_element_type=jnp.float32
        )


def terms_kernel(cells_ref, grad_ref, order_ref, part_ref, out_ref, held_ref, sems):
    turned = turned_grad(grad_ref, order_ref)
    copies = []
    for start in range(0, 9, 2):
        some = TAPS[start : start + 2]
        cells = jnp.concatenate([block_of(cells_ref, a, b) for a, b in some], axis=1)
        terms = jnp.dot(turned, cells, preferred_element_type=jnp.float32)
        terms += part_ref[:, start * 128 : (start + len(some)) * 128]
        terms = terms.astype(jnp.bfloat16)
        for i in range(len(some)):
            for c in range(3):
                tap = (start + i) * 3 + c
                held_ref[:, tap * 128 : (tap + 1) * 128] = terms[
                    c * 256 : (c + 1) * 256, i * 128 : (i + 1) * 128
                ]
        lanes = pl.ds(start * 384, len(some) * 384)
        copy = pltpu.make_async_copy(
            held_ref.at[:, lanes], out_ref.at[:, lanes], sems.at[start // 2]
        )
        copy.start()
        copies.append(copy)
    for copy in copies:
        copy.wait()


def plane_kernel(got_ref, out_ref):
    total = got_ref[0].astype(jnp.float32)
    for i in range(1, 16):
        total += got_ref[i].astype(jnp.float32)
    for z in range(8):
        out_ref[z] = total[2 * z : 2 * z + 2].astype(out_ref.dtype)


def line_kernel(got_ref, out_ref):
    total = got_ref[0].astype(jnp.float32)
    for i in range(1, 8):
        total += got_ref[i].astype(jnp.float32)
    total *= 1.0 / math.sqrt(32.0 * 32.0 * 128.0)
    for i in range(8):
        out_ref[i] = total


def share_kernel(mine_ref, other_ref, out_ref):
    core = lax.axis_index("tm") % 2
    for tap in range(27):
        lanes = slice(tap * 128, (tap + 1) * 128)
        mine = jnp.concatenate([mine_ref[q, :, lanes] for q in range(8)], axis=0)
        other = jnp.concatenate([other_ref[q, :, lanes] for q in range(8)], axis=0)
        out_ref[tap] = jnp.where(
            core == 0,
            jnp.concatenate([mine, other], axis=1),
            jnp.concatenate([other, mine], axis=1),
        )


def call(kernel, shapes, flops):
    return pl.pallas_call(
        kernel,
        out_shape=shapes,
        compiler_params=VMEM,
        cost_estimate=pl.CostEstimate(flops=flops, bytes_accessed=5000000, transcendentals=0),
    )


def row_order():
    channels = np.arange(256).reshape(2, 8, 8, 2).transpose(0, 2, 1, 3).reshape(256)
    return (channels[:, None] == np.arange(256)[None, :]).astype(np.float32)


def local(frames_in, weight, cotangent):
    core = lax.axis_index("tm") % 2
    block = jax.ShapeDtypeStruct((2, 2, 128, 256), jnp.bfloat16)
    flops = 2 * 512 * 6912 * 256

    carried = shifted(frames_in, "tm", 1)
    even = lax.axis_index("space") % 2 == 0
    edge = jax.ShapeDtypeStruct((2, 1, 128, 256), jnp.bfloat16)
    top, bottom, own = call(edge_kernel, (edge, edge, block), 100000)(frames_in)
    near, far = row_halo(
        jnp.concatenate([carried[:, :1], top], axis=0),
        jnp.concatenate([carried[:, 1:], bottom], axis=0),
    )
    part = pl.pallas_call(
        near_kernel,
        out_shape=jax.ShapeDtypeStruct((4, 128, 256), jnp.float32),
        in_specs=[
            pl.BlockSpec(memory_space=pltpu.VMEM),
            pl.BlockSpec(memory_space=pltpu.VMEM),
            pl.BlockSpec(memory_space=pltpu.HBM),
        ],
        scratch_shapes=[
            pltpu.VMEM((3, 3, 3, 256, 256), jnp.bfloat16),
            pltpu.SemaphoreType.DMA((3,)),
        ],
        compiler_params=pltpu.CompilerParams(vmem_limit_bytes=50 * 1024 * 1024),
        cost_estimate=pl.CostEstimate(flops=flops, bytes_accessed=5000000, transcendentals=0),
    )(carried, own, weight)
    near, far, part = lax.optimization_barrier((near, far, part))
    before, after = jnp.where(even, far, near), jnp.where(even, near, far)
    ext = jnp.concatenate(
        [before, jnp.concatenate([carried, own], axis=0), after], axis=1
    )
    low, high = ext[..., :128], ext[..., 128:]
    mine = jnp.where(core == 0, low, high)
    theirs = flip_core(jnp.where(core == 0, high, low))
    output, grad_pre = call(forward_kernel, (block, block), flops // 3)(
        before, after, own, part, weight, cotangent
    )
    grad_other = flip_core(grad_pre)
    order = jnp.asarray(row_order(), jnp.bfloat16)
    own_terms = call(own_terms_kernel, jax.ShapeDtypeStruct((768, 1152), jnp.float32), flops // 2)(
        mine, grad_pre, order
    )
    terms = pl.pallas_call(
        terms_kernel,
        out_shape=jax.ShapeDtypeStruct((256, 3456), jnp.bfloat16),
        out_specs=pl.BlockSpec(memory_space=pl.ANY),
        scratch_shapes=[pltpu.VMEM((256, 3456), jnp.bfloat16), pltpu.SemaphoreType.DMA((5,))],
        compiler_params=VMEM,
        cost_estimate=pl.CostEstimate(flops=flops // 2, bytes_accessed=5000000, transcendentals=0),
    )(theirs, grad_other, order, own_terms)
    near, far = row_halo(grad_pre[:, :1], grad_pre[:, 1:])
    above, below = jnp.where(even, far, near), jnp.where(even, near, far)
    tall = jnp.concatenate([above, grad_pre, below], axis=1)
    follow = shifted(tall, "tm", -1)
    got = exchange(terms, ("x_lo", "x_hi", "y")).reshape(16, 16, 3456)
    plane = pl.pallas_call(
        plane_kernel,
        out_shape=jax.ShapeDtypeStruct((8, 2, 3456), jnp.bfloat16),
        grid=(3,),
        in_specs=[pl.BlockSpec((16, 16, 1152), lambda i: (0, 0, i))],
        out_specs=pl.BlockSpec((8, 2, 1152), lambda i: (0, 0, i)),
        compiler_params=VMEM,
    )(got)
    got = exchange(plane, ("z",)).reshape(8, 2, 3456)
    copies = call(line_kernel, jax.ShapeDtypeStruct((8, 2, 3456), jnp.float32), 100000)(got)
    copies, tall, follow = lax.optimization_barrier((copies, tall, follow))
    grad_ext = jnp.concatenate([tall, follow], axis=0)
    share = exchange(copies, ("x_hi", "y")).reshape(8, 2, 3456)
    grad_input = call(backward_kernel, block, flops)(grad_ext, weight, cotangent)
    share, grad_input = lax.optimization_barrier((share, grad_input))
    other = flip_core(share)
    share = call(share_kernel, jax.ShapeDtypeStruct((27, 16, 256), jnp.float32), 100000)(
        share, other
    )
    grad_weight = share.transpose(1, 0, 2).reshape(16, 3, 3, 3, 256)
    return (output, grad_input, grad_weight)


def solution(mesh):
    placed = (P("tm", "space", None, None), P(), P("tm", "space", None, None))
    return jax.shard_map(
        local,
        mesh=mesh,
        in_specs=placed,
        out_specs=(
            P("tm", "space", None, None),
            P("tm", "space", None, None),
            P("space", None, None, None, None),
        ),
        check_vma=False,
    )
```

```python
import functools
import itertools
import math

import jax
import jax.numpy as jnp
import numpy as np
from jax import lax
from jax.experimental import pallas as pl
from jax.experimental.pallas import tpu as pltpu
from jax.sharding import PartitionSpec as P

BOTH = ("tm", "space")
VMEM = pltpu.CompilerParams(vmem_limit_bytes=20 * 1024 * 1024)
SIZES = {"x_hi": 2, "y": 4, "core": 2, "x_lo": 2, "z": 8}


def groups_of(names):
    rest = [n for n in SIZES if n not in names]
    groups = []
    for fixed in itertools.product(*(range(SIZES[n]) for n in rest)):
        group = []
        for varied in itertools.product(*(range(SIZES[n]) for n in names)):
            at = dict(zip(rest, fixed)) | dict(zip(names, varied))
            tm = (at["x_hi"] * 4 + at["y"]) * 2 + at["core"]
            group.append(tm * 16 + at["x_lo"] * 8 + at["z"])
        groups.append(group)
    return groups


def exchange(value, names):
    return lax.all_to_all(value, BOTH, 0, 0, tiled=True, axis_index_groups=groups_of(names))


def flip_core(value):
    return lax.ppermute(value, "tm", [(i, i ^ 1) for i in range(16)])


def shifted(value, axis, steps):
    count = lax.axis_size(axis)
    leading, last = (max(0, -steps), min(count, count - steps))
    return lax.ppermute(value, axis, [(source, source + steps) for source in range(leading, last)])


def pairs(value, first):
    links = [(i, i + 1) for i in range(first, 15, 2)]
    return lax.ppermute(value, "space", links + [(j, i) for i, j in links])


def row_halo(top, bottom):
    even = lax.axis_index("space") % 2 == 0
    near = pairs(jnp.where(even, bottom, top), 0)
    far = pairs(jnp.where(even, top, bottom), 1)
    return near, far


def shift_cols(value, steps):
    zero = jnp.zeros_like(value[:, :1])
    if steps == 1:
        return jnp.concatenate([zero, value[:, :-1]], axis=1)
    return jnp.concatenate([value[:, 1:], zero], axis=1)


def block_of(ref, a, b):
    return ref[a : a + 2, b : b + 2].reshape(512, -1)


def edge_kernel(frames_ref, top_ref, bottom_ref, own_ref):
    top_ref[...] = frames_ref[:, :1]
    bottom_ref[...] = frames_ref[:, 1:]
    own_ref[...] = frames_ref[...]


def near_kernel(carried_ref, own_ref, w_from, part_ref, w_ref, sems):
    copies = [
        pltpu.make_async_copy(w_from.at[:, :, c], w_ref.at[:, :, c], sems.at[c]) for c in range(3)
    ]
    for copy in copies:
        copy.start()
    blocks = [
        carried_ref[...],
        jnp.concatenate([carried_ref[1:], own_ref[:1]], axis=0),
        own_ref[...],
    ]
    sums = []
    for c in range(3):
        both = jnp.zeros((512, 256), jnp.float32)
        upper = jnp.zeros((256, 256), jnp.float32)
        lower = jnp.zeros((256, 256), jnp.float32)
        copies[c].wait()
        for a in range(3):
            rows = [blocks[a][:, r].reshape(256, 256) for r in range(2)]
            both += jnp.dot(
                jnp.concatenate(rows, axis=0), w_ref[a, 1, c], preferred_element_type=jnp.float32
            )
            upper += jnp.dot(rows[1], w_ref[a, 2, c], preferred_element_type=jnp.float32)
            lower += jnp.dot(rows[0], w_ref[a, 0, c], preferred_element_type=jnp.float32)
        sums.append((both + jnp.concatenate([upper, lower], axis=0)).reshape(4, 128, 256))
    part_ref[...] = shift_cols(sums[0], 1) + sums[1] + shift_cols(sums[2], -1)


def forward_kernel(before_ref, after_ref, own_ref, part_ref, w_ref, cot_ref, out_ref, grad_ref):
    sums = []
    for c in range(3):
        upper = jnp.zeros((256, 256), jnp.float32)
        lower = jnp.zeros((256, 256), jnp.float32)
        for a in range(3):
            top = before_ref[a : a + 2].reshape(256, 256)
            bottom = after_ref[a : a + 2].reshape(256, 256)
            upper += jnp.dot(top, w_ref[a, 0, c], preferred_element_type=jnp.float32)
            lower += jnp.dot(bottom, w_ref[a, 2, c], preferred_element_type=jnp.float32)
        sums.append(jnp.concatenate([upper, lower], axis=0).reshape(4, 128, 256))
    total = part_ref[...] + shift_cols(sums[0], 1) + sums[1] + shift_cols(sums[2], -1)
    for row in range(2):
        preact = total[2 * row : 2 * row + 2]
        own = own_ref[:, row].astype(jnp.float32)
        sigma = 1.0 / (1.0 + jnp.exp(-preact))
        out_ref[:, row] = (own + preact * sigma).astype(jnp.bfloat16)
        cot = cot_ref[:, row].astype(jnp.float32)
        grad = cot * sigma * (1.0 + preact * (1.0 - sigma))
        grad_ref[:, row] = grad.astype(jnp.bfloat16)


def backward_kernel(ext_ref, w_ref, cot_ref, out_ref):
    sums = []
    for c in range(3):
        acc = jnp.zeros((512, 256), jnp.float32)
        for a in range(3):
            for b in range(3):
                acc += lax.dot_general(
                    block_of(ext_ref, 2 - a, 2 - b),
                    w_ref[a, b, c],
                    (((1,), (1,)), ((), ())),
                    preferred_element_type=jnp.float32,
                )
        sums.append(acc.reshape(4, 128, 256))
    total = shift_cols(sums[0], -1) + sums[1] + shift_cols(sums[2], 1)
    cot = cot_ref[...].reshape(4, 128, 256).astype(jnp.float32)
    out_ref[...] = (cot + total).astype(jnp.bfloat16).reshape(2, 2, 128, 256)


def turned_grad(grad_ref, order_ref):
    parts = []
    for steps in (-1, 0, 1):
        value = grad_ref[...].reshape(4, 128, 256)
        if steps:
            value = shift_cols(value.astype(jnp.float32), steps).astype(jnp.bfloat16)
        turned = lax.dot_general(
            order_ref[...],
            value.reshape(512, 256),
            (((1,), (1,)), ((), ())),
            preferred_element_type=jnp.float32,
        )
        parts.append(turned.astype(jnp.bfloat16))
    return jnp.concatenate(parts, axis=0)


TAPS = [(a, b) for a in range(3) for b in range(3)]


def own_terms_kernel(cells_ref, grad_ref, order_ref, out_ref):
    turned = turned_grad(grad_ref, order_ref)
    for start in range(0, 9, 2):
        some = TAPS[start : start + 2]
        cells = jnp.concatenate([block_of(cells_ref, a, b) for a, b in some], axis=1)
        out_ref[:, start * 128 : (start + len(some)) * 128] = jnp.dot(
            turned, cells, preferred_element_type=jnp.float32
        )


def terms_kernel(cells_ref, grad_ref, order_ref, part_ref, out_ref, held_ref, sems):
    turned = turned_grad(grad_ref, order_ref)
    copies = []
    for start in range(0, 9, 2):
        some = TAPS[start : start + 2]
        cells = jnp.concatenate([block_of(cells_ref, a, b) for a, b in some], axis=1)
        terms = jnp.dot(turned, cells, preferred_element_type=jnp.float32)
        terms += part_ref[:, start * 128 : (start + len(some)) * 128]
        terms = terms.astype(jnp.bfloat16)
        for i in range(len(some)):
            for c in range(3):
                tap = (start + i) * 3 + c
                held_ref[:, tap * 128 : (tap + 1) * 128] = terms[
                    c * 256 : (c + 1) * 256, i * 128 : (i + 1) * 128
                ]
        lanes = pl.ds(start * 384, len(some) * 384)
        copy = pltpu.make_async_copy(
            held_ref.at[:, lanes], out_ref.at[:, lanes], sems.at[start // 2]
        )
        copy.start()
        copies.append(copy)
    for copy in copies:
        copy.wait()


def plane_kernel(got_ref, out_ref):
    total = got_ref[0].astype(jnp.float32)
    for i in range(1, 16):
        total += got_ref[i].astype(jnp.float32)
    for z in range(8):
        out_ref[z] = total[2 * z : 2 * z + 2].astype(out_ref.dtype)


def line_kernel(got_ref, out_ref):
    total = got_ref[0].astype(jnp.float32)
    for i in range(1, 8):
        total += got_ref[i].astype(jnp.float32)
    total *= 1.0 / math.sqrt(32.0 * 32.0 * 128.0)
    for i in range(8):
        out_ref[i] = total


def share_kernel(mine_ref, other_ref, out_ref):
    core = lax.axis_index("tm") % 2
    for tap in range(27):
        lanes = slice(tap * 128, (tap + 1) * 128)
        mine = jnp.concatenate([mine_ref[q, :, lanes] for q in range(8)], axis=0)
        other = jnp.concatenate([other_ref[q, :, lanes] for q in range(8)], axis=0)
        out_ref[tap] = jnp.where(
            core == 0,
            jnp.concatenate([mine, other], axis=1),
            jnp.concatenate([other, mine], axis=1),
        )


def call(kernel, shapes, flops):
    return pl.pallas_call(
        kernel,
        out_shape=shapes,
        compiler_params=VMEM,
        cost_estimate=pl.CostEstimate(flops=flops, bytes_accessed=5000000, transcendentals=0),
    )


def row_order():
    channels = np.arange(256).reshape(2, 8, 8, 2).transpose(0, 2, 1, 3).reshape(256)
    return (channels[:, None] == np.arange(256)[None, :]).astype(np.float32)


def local(frames_in, weight, cotangent):
    core = lax.axis_index("tm") % 2
    block = jax.ShapeDtypeStruct((2, 2, 128, 256), jnp.bfloat16)
    flops = 2 * 512 * 6912 * 256

    carried = shifted(frames_in, "tm", 1)
    even = lax.axis_index("space") % 2 == 0
    edge = jax.ShapeDtypeStruct((2, 1, 128, 256), jnp.bfloat16)
    top, bottom, own = call(edge_kernel, (edge, edge, block), 100000)(frames_in)
    near, far = row_halo(
        jnp.concatenate([carried[:, :1], top], axis=0),
        jnp.concatenate([carried[:, 1:], bottom], axis=0),
    )
    part = pl.pallas_call(
        near_kernel,
        out_shape=jax.ShapeDtypeStruct((4, 128, 256), jnp.float32),
        in_specs=[
            pl.BlockSpec(memory_space=pltpu.VMEM),
            pl.BlockSpec(memory_space=pltpu.VMEM),
            pl.BlockSpec(memory_space=pltpu.HBM),
        ],
        scratch_shapes=[
            pltpu.VMEM((3, 3, 3, 256, 256), jnp.bfloat16),
            pltpu.SemaphoreType.DMA((3,)),
        ],
        compiler_params=pltpu.CompilerParams(vmem_limit_bytes=50 * 1024 * 1024),
        cost_estimate=pl.CostEstimate(flops=flops, bytes_accessed=5000000, transcendentals=0),
    )(carried, own, weight)
    near, far, part = lax.optimization_barrier((near, far, part))
    before, after = jnp.where(even, far, near), jnp.where(even, near, far)
    ext = jnp.concatenate(
        [before, jnp.concatenate([carried, own], axis=0), after], axis=1
    )
    low, high = ext[..., :128], ext[..., 128:]
    mine = jnp.where(core == 0, low, high)
    theirs = flip_core(jnp.where(core == 0, high, low))
    output, grad_pre = call(forward_kernel, (block, block), flops // 3)(
        before, after, own, part, weight, cotangent
    )
    grad_other = flip_core(grad_pre)
    order = jnp.asarray(row_order(), jnp.bfloat16)
    own_terms = call(own_terms_kernel, jax.ShapeDtypeStruct((768, 1152), jnp.float32), flops // 2)(
        mine, grad_pre, order
    )
    terms = pl.pallas_call(
        terms_kernel,
        out_shape=jax.ShapeDtypeStruct((256, 3456), jnp.bfloat16),
        out_specs=pl.BlockSpec(memory_space=pl.ANY),
        scratch_shapes=[pltpu.VMEM((256, 3456), jnp.bfloat16), pltpu.SemaphoreType.DMA((5,))],
        compiler_params=VMEM,
        cost_estimate=pl.CostEstimate(flops=flops // 2, bytes_accessed=5000000, transcendentals=0),
    )(theirs, grad_other, order, own_terms)
    near, far = row_halo(grad_pre[:, :1], grad_pre[:, 1:])
    above, below = jnp.where(even, far, near), jnp.where(even, near, far)
    tall = jnp.concatenate([above, grad_pre, below], axis=1)
    follow = shifted(tall, "tm", -1)
    got = exchange(terms, ("x_lo", "x_hi", "y")).reshape(16, 16, 3456)
    plane = pl.pallas_call(
        plane_kernel,
        out_shape=jax.ShapeDtypeStruct((8, 2, 3456), jnp.bfloat16),
        grid=(3,),
        in_specs=[pl.BlockSpec((16, 16, 1152), lambda i: (0, 0, i))],
        out_specs=pl.BlockSpec((8, 2, 1152), lambda i: (0, 0, i)),
        compiler_params=VMEM,
    )(got)
    got = exchange(plane, ("z",)).reshape(8, 2, 3456)
    tall, follow, _ = lax.optimization_barrier((tall, follow, plane))
    grad_ext = jnp.concatenate([tall, follow], axis=0)
    grad_input = call(backward_kernel, block, flops)(grad_ext, weight, cotangent)
    got, grad_input = lax.optimization_barrier((got, grad_input))
    copies = call(line_kernel, jax.ShapeDtypeStruct((8, 2, 3456), jnp.float32), 100000)(got)
    share = exchange(copies, ("x_hi", "y")).reshape(8, 2, 3456)
    other = flip_core(share)
    share = call(share_kernel, jax.ShapeDtypeStruct((27, 16, 256), jnp.float32), 100000)(
        share, other
    )
    grad_weight = share.transpose(1, 0, 2).reshape(16, 3, 3, 3, 256)
    return (output, grad_input, grad_weight)


def solution(mesh):
    placed = (P("tm", "space", None, None), P(), P("tm", "space", None, None))
    return jax.shard_map(
        local,
        mesh=mesh,
        in_specs=placed,
        out_specs=(
            P("tm", "space", None, None),
            P("tm", "space", None, None),
            P("space", None, None, None, None),
        ),
        check_vma=False,
    )
```

```python
import functools
import itertools
import math

import jax
import jax.numpy as jnp
import numpy as np
from jax import lax
from jax.experimental import pallas as pl
from jax.experimental.pallas import tpu as pltpu
from jax.sharding import PartitionSpec as P

BOTH = ("tm", "space")
VMEM = pltpu.CompilerParams(vmem_limit_bytes=20 * 1024 * 1024)
SIZES = {"x_hi": 2, "y": 4, "core": 2, "x_lo": 2, "z": 8}


def groups_of(names):
    rest = [n for n in SIZES if n not in names]
    groups = []
    for fixed in itertools.product(*(range(SIZES[n]) for n in rest)):
        group = []
        for varied in itertools.product(*(range(SIZES[n]) for n in names)):
            at = dict(zip(rest, fixed)) | dict(zip(names, varied))
            tm = (at["x_hi"] * 4 + at["y"]) * 2 + at["core"]
            group.append(tm * 16 + at["x_lo"] * 8 + at["z"])
        groups.append(group)
    return groups


def exchange(value, names):
    return lax.all_to_all(value, BOTH, 0, 0, tiled=True, axis_index_groups=groups_of(names))


def flip_core(value):
    return lax.ppermute(value, "tm", [(i, i ^ 1) for i in range(16)])


def shifted(value, axis, steps):
    count = lax.axis_size(axis)
    leading, last = (max(0, -steps), min(count, count - steps))
    return lax.ppermute(value, axis, [(source, source + steps) for source in range(leading, last)])


def pairs(value, first):
    links = [(i, i + 1) for i in range(first, 15, 2)]
    return lax.ppermute(value, "space", links + [(j, i) for i, j in links])


def row_halo(top, bottom):
    even = lax.axis_index("space") % 2 == 0
    near = pairs(jnp.where(even, bottom, top), 0)
    far = pairs(jnp.where(even, top, bottom), 1)
    return near, far


def shift_cols(value, steps):
    zero = jnp.zeros_like(value[:, :1])
    if steps == 1:
        return jnp.concatenate([zero, value[:, :-1]], axis=1)
    return jnp.concatenate([value[:, 1:], zero], axis=1)


def block_of(ref, a, b):
    return ref[a : a + 2, b : b + 2].reshape(512, -1)


def edge_kernel(frames_ref, top_ref, bottom_ref, own_ref):
    top_ref[...] = frames_ref[:, :1]
    bottom_ref[...] = frames_ref[:, 1:]
    own_ref[...] = frames_ref[...]


def near_kernel(carried_ref, own_ref, w_ref, part_ref, held_ref):
    held_ref[:, 0] = w_ref[:, 0]
    held_ref[:, 1] = w_ref[:, 2]
    blocks = [
        carried_ref[...],
        jnp.concatenate([carried_ref[1:], own_ref[:1]], axis=0),
        own_ref[...],
    ]
    sums = []
    for c in range(3):
        both = jnp.zeros((512, 256), jnp.float32)
        upper = jnp.zeros((256, 256), jnp.float32)
        lower = jnp.zeros((256, 256), jnp.float32)
        for a in range(3):
            rows = [blocks[a][:, r].reshape(256, 256) for r in range(2)]
            both += jnp.dot(
                jnp.concatenate(rows, axis=0), w_ref[a, 1, c], preferred_element_type=jnp.float32
            )
            upper += jnp.dot(rows[1], w_ref[a, 2, c], preferred_element_type=jnp.float32)
            lower += jnp.dot(rows[0], w_ref[a, 0, c], preferred_element_type=jnp.float32)
        sums.append((both + jnp.concatenate([upper, lower], axis=0)).reshape(4, 128, 256))
    part_ref[...] = shift_cols(sums[0], 1) + sums[1] + shift_cols(sums[2], -1)


def forward_kernel(near_ref, far_ref, own_ref, part_ref, w_ref, cot_ref, out_ref, grad_ref):
    even = lax.axis_index("space") % 2 == 0
    near, far = near_ref[...].reshape(4, 128, 256), far_ref[...].reshape(4, 128, 256)
    above, below = jnp.where(even, far, near), jnp.where(even, near, far)
    sums = []
    for c in range(3):
        upper = jnp.zeros((256, 256), jnp.float32)
        lower = jnp.zeros((256, 256), jnp.float32)
        for a in range(3):
            top = above[a : a + 2].reshape(256, 256)
            bottom = below[a : a + 2].reshape(256, 256)
            upper += jnp.dot(top, w_ref[a, 0, c], preferred_element_type=jnp.float32)
            lower += jnp.dot(bottom, w_ref[a, 1, c], preferred_element_type=jnp.float32)
        sums.append(jnp.concatenate([upper, lower], axis=0).reshape(4, 128, 256))
    total = part_ref[...] + shift_cols(sums[0], 1) + sums[1] + shift_cols(sums[2], -1)
    for row in range(2):
        preact = total[2 * row : 2 * row + 2]
        own = own_ref[:, row].astype(jnp.float32)
        sigma = 1.0 / (1.0 + jnp.exp(-preact))
        out_ref[:, row] = (own + preact * sigma).astype(jnp.bfloat16)
        cot = cot_ref[:, row].astype(jnp.float32)
        grad = cot * sigma * (1.0 + preact * (1.0 - sigma))
        grad_ref[:, row] = grad.astype(jnp.bfloat16)


def backward_kernel(ext_ref, w_ref, cot_ref, out_ref):
    sums = []
    for c in range(3):
        acc = jnp.zeros((512, 256), jnp.float32)
        for a in range(3):
            for b in range(3):
                acc += lax.dot_general(
                    block_of(ext_ref, 2 - a, 2 - b),
                    w_ref[a, b, c],
                    (((1,), (1,)), ((), ())),
                    preferred_element_type=jnp.float32,
                )
        sums.append(acc.reshape(4, 128, 256))
    total = shift_cols(sums[0], -1) + sums[1] + shift_cols(sums[2], 1)
    cot = cot_ref[...].reshape(4, 128, 256).astype(jnp.float32)
    out_ref[...] = (cot + total).astype(jnp.bfloat16).reshape(2, 2, 128, 256)


def turned_grad(grad_ref, order_ref):
    parts = []
    for steps in (-1, 0, 1):
        value = grad_ref[...].reshape(4, 128, 256)
        if steps:
            value = shift_cols(value.astype(jnp.float32), steps).astype(jnp.bfloat16)
        turned = lax.dot_general(
            order_ref[...],
            value.reshape(512, 256),
            (((1,), (1,)), ((), ())),
            preferred_element_type=jnp.float32,
        )
        parts.append(turned.astype(jnp.bfloat16))
    return jnp.concatenate(parts, axis=0)


TAPS = [(a, b) for a in range(3) for b in range(3)]


def own_terms_kernel(cells_ref, grad_ref, order_ref, out_ref):
    turned = turned_grad(grad_ref, order_ref)
    for start in range(0, 9, 2):
        some = TAPS[start : start + 2]
        cells = jnp.concatenate([block_of(cells_ref, a, b) for a, b in some], axis=1)
        out_ref[:, start * 128 : (start + len(some)) * 128] = jnp.dot(
            turned, cells, preferred_element_type=jnp.float32
        )


def terms_kernel(cells_ref, grad_ref, order_ref, part_ref, out_ref, held_ref, sems):
    turned = turned_grad(grad_ref, order_ref)
    copies = []
    for start in range(0, 9, 2):
        some = TAPS[start : start + 2]
        cells = jnp.concatenate([block_of(cells_ref, a, b) for a, b in some], axis=1)
        terms = jnp.dot(turned, cells, preferred_element_type=jnp.float32)
        terms += part_ref[:, start * 128 : (start + len(some)) * 128]
        terms = terms.astype(jnp.bfloat16)
        for i in range(len(some)):
            for c in range(3):
                tap = (start + i) * 3 + c
                held_ref[:, tap * 128 : (tap + 1) * 128] = terms[
                    c * 256 : (c + 1) * 256, i * 128 : (i + 1) * 128
                ]
        lanes = pl.ds(start * 384, len(some) * 384)
        copy = pltpu.make_async_copy(
            held_ref.at[:, lanes], out_ref.at[:, lanes], sems.at[start // 2]
        )
        copy.start()
        copies.append(copy)
    for copy in copies:
        copy.wait()


def plane_kernel(got_ref, out_ref):
    total = got_ref[0].astype(jnp.float32)
    for i in range(1, 16):
        total += got_ref[i].astype(jnp.float32)
    for z in range(8):
        out_ref[z] = total[2 * z : 2 * z + 2].astype(out_ref.dtype)


def line_kernel(got_ref, out_ref):
    total = got_ref[0].astype(jnp.float32)
    for i in range(1, 8):
        total += got_ref[i].astype(jnp.float32)
    total *= 1.0 / math.sqrt(32.0 * 32.0 * 128.0)
    for i in range(8):
        out_ref[i] = total


def share_kernel(mine_ref, other_ref, out_ref):
    core = lax.axis_index("tm") % 2
    for tap in range(27):
        lanes = slice(tap * 128, (tap + 1) * 128)
        mine = jnp.concatenate([mine_ref[q, :, lanes] for q in range(8)], axis=0)
        other = jnp.concatenate([other_ref[q, :, lanes] for q in range(8)], axis=0)
        out_ref[tap] = jnp.where(
            core == 0,
            jnp.concatenate([mine, other], axis=1),
            jnp.concatenate([other, mine], axis=1),
        )


def call(kernel, shapes, flops):
    return pl.pallas_call(
        kernel,
        out_shape=shapes,
        compiler_params=VMEM,
        cost_estimate=pl.CostEstimate(flops=flops, bytes_accessed=5000000, transcendentals=0),
    )


def row_order():
    channels = np.arange(256).reshape(2, 8, 8, 2).transpose(0, 2, 1, 3).reshape(256)
    return (channels[:, None] == np.arange(256)[None, :]).astype(np.float32)


def local(frames_in, weight, cotangent):
    core = lax.axis_index("tm") % 2
    block = jax.ShapeDtypeStruct((2, 2, 128, 256), jnp.bfloat16)
    flops = 2 * 512 * 6912 * 256

    carried = shifted(frames_in, "tm", 1)
    even = lax.axis_index("space") % 2 == 0
    edge = jax.ShapeDtypeStruct((2, 1, 128, 256), jnp.bfloat16)
    top, bottom, own = call(edge_kernel, (edge, edge, block), 100000)(frames_in)
    near, far = row_halo(
        jnp.concatenate([carried[:, :1], top], axis=0),
        jnp.concatenate([carried[:, 1:], bottom], axis=0),
    )
    part, held = call(
        near_kernel,
        (
            jax.ShapeDtypeStruct((4, 128, 256), jnp.float32),
            jax.ShapeDtypeStruct((3, 2, 3, 256, 256), jnp.bfloat16),
        ),
        flops,
    )(carried, own, weight)
    near, far, part = lax.optimization_barrier((near, far, part))
    output, grad_pre = call(forward_kernel, (block, block), flops // 3)(
        near, far, own, part, held, cotangent
    )
    near, far, grad_pre = lax.optimization_barrier((near, far, grad_pre))
    grad_other = flip_core(grad_pre)
    before, after = jnp.where(even, far, near), jnp.where(even, near, far)
    ext = jnp.concatenate(
        [before, jnp.concatenate([carried, own], axis=0), after], axis=1
    )
    low, high = ext[..., :128], ext[..., 128:]
    mine = jnp.where(core == 0, low, high)
    theirs = flip_core(jnp.where(core == 0, high, low))
    order = jnp.asarray(row_order(), jnp.bfloat16)
    own_terms = call(own_terms_kernel, jax.ShapeDtypeStruct((768, 1152), jnp.float32), flops // 2)(
        mine, grad_pre, order
    )
    terms = pl.pallas_call(
        terms_kernel,
        out_shape=jax.ShapeDtypeStruct((256, 3456), jnp.bfloat16),
        out_specs=pl.BlockSpec(memory_space=pl.ANY),
        scratch_shapes=[pltpu.VMEM((256, 3456), jnp.bfloat16), pltpu.SemaphoreType.DMA((5,))],
        compiler_params=VMEM,
        cost_estimate=pl.CostEstimate(flops=flops // 2, bytes_accessed=5000000, transcendentals=0),
    )(theirs, grad_other, order, own_terms)
    near, far = row_halo(grad_pre[:, :1], grad_pre[:, 1:])
    above, below = jnp.where(even, far, near), jnp.where(even, near, far)
    tall = jnp.concatenate([above, grad_pre, below], axis=1)
    follow = shifted(tall, "tm", -1)
    got = exchange(terms, ("x_lo", "x_hi", "y")).reshape(16, 16, 3456)
    plane = pl.pallas_call(
        plane_kernel,
        out_shape=jax.ShapeDtypeStruct((8, 2, 3456), jnp.bfloat16),
        grid=(3,),
        in_specs=[pl.BlockSpec((16, 16, 1152), lambda i: (0, 0, i))],
        out_specs=pl.BlockSpec((8, 2, 1152), lambda i: (0, 0, i)),
        compiler_params=VMEM,
    )(got)
    got = exchange(plane, ("z",)).reshape(8, 2, 3456)
    copies = call(line_kernel, jax.ShapeDtypeStruct((8, 2, 3456), jnp.float32), 100000)(got)
    copies, tall, follow = lax.optimization_barrier((copies, tall, follow))
    grad_ext = jnp.concatenate([tall, follow], axis=0)
    share = exchange(copies, ("x_hi", "y")).reshape(8, 2, 3456)
    grad_input = call(backward_kernel, block, flops)(grad_ext, weight, cotangent)
    share, grad_input = lax.optimization_barrier((share, grad_input))
    other = flip_core(share)
    share = call(share_kernel, jax.ShapeDtypeStruct((27, 16, 256), jnp.float32), 100000)(
        share, other
    )
    grad_weight = share.transpose(1, 0, 2).reshape(16, 3, 3, 3, 256)
    return (output, grad_input, grad_weight)


def solution(mesh):
    placed = (P("tm", "space", None, None), P(), P("tm", "space", None, None))
    return jax.shard_map(
        local,
        mesh=mesh,
        in_specs=placed,
        out_specs=(
            P("tm", "space", None, None),
            P("tm", "space", None, None),
            P("space", None, None, None, None),
        ),
        check_vma=False,
    )
```

```python
import functools
import itertools
import math

import jax
import jax.numpy as jnp
import numpy as np
from jax import lax
from jax.experimental import pallas as pl
from jax.experimental.pallas import tpu as pltpu
from jax.sharding import PartitionSpec as P

BOTH = ("tm", "space")
VMEM = pltpu.CompilerParams(vmem_limit_bytes=20 * 1024 * 1024)
SIZES = {"x_hi": 2, "y": 4, "core": 2, "x_lo": 2, "z": 8}


def groups_of(names):
    rest = [n for n in SIZES if n not in names]
    groups = []
    for fixed in itertools.product(*(range(SIZES[n]) for n in rest)):
        group = []
        for varied in itertools.product(*(range(SIZES[n]) for n in names)):
            at = dict(zip(rest, fixed)) | dict(zip(names, varied))
            tm = (at["x_hi"] * 4 + at["y"]) * 2 + at["core"]
            group.append(tm * 16 + at["x_lo"] * 8 + at["z"])
        groups.append(group)
    return groups


def exchange(value, names):
    return lax.all_to_all(value, BOTH, 0, 0, tiled=True, axis_index_groups=groups_of(names))


def flip_core(value):
    return lax.ppermute(value, "tm", [(i, i ^ 1) for i in range(16)])


def shifted(value, axis, steps):
    count = lax.axis_size(axis)
    leading, last = (max(0, -steps), min(count, count - steps))
    return lax.ppermute(value, axis, [(source, source + steps) for source in range(leading, last)])


def pairs(value, first):
    links = [(i, i + 1) for i in range(first, 15, 2)]
    return lax.ppermute(value, "space", links + [(j, i) for i, j in links])


def row_halo(top, bottom):
    even = lax.axis_index("space") % 2 == 0
    near = pairs(jnp.where(even, bottom, top), 0)
    far = pairs(jnp.where(even, top, bottom), 1)
    return near, far


def shift_cols(value, steps):
    zero = jnp.zeros_like(value[:, :1])
    if steps == 1:
        return jnp.concatenate([zero, value[:, :-1]], axis=1)
    return jnp.concatenate([value[:, 1:], zero], axis=1)


def block_of(ref, a, b):
    return ref[a : a + 2, b : b + 2].reshape(512, -1)


def edge_kernel(frames_ref, top_ref, bottom_ref, own_ref):
    top_ref[...] = frames_ref[:, :1]
    bottom_ref[...] = frames_ref[:, 1:]
    own_ref[...] = frames_ref[...]


def near_kernel(carried_ref, own_ref, w_ref, part_ref, held_ref):
    held_ref[:, 0] = w_ref[:, 0]
    held_ref[:, 1] = w_ref[:, 2]
    blocks = [
        carried_ref[...],
        jnp.concatenate([carried_ref[1:], own_ref[:1]], axis=0),
        own_ref[...],
    ]
    sums = []
    for c in range(3):
        both = jnp.zeros((512, 256), jnp.float32)
        upper = jnp.zeros((256, 256), jnp.float32)
        lower = jnp.zeros((256, 256), jnp.float32)
        for a in range(3):
            rows = [blocks[a][:, r].reshape(256, 256) for r in range(2)]
            both += jnp.dot(
                jnp.concatenate(rows, axis=0), w_ref[a, 1, c], preferred_element_type=jnp.float32
            )
            upper += jnp.dot(rows[1], w_ref[a, 2, c], preferred_element_type=jnp.float32)
            lower += jnp.dot(rows[0], w_ref[a, 0, c], preferred_element_type=jnp.float32)
        sums.append((both + jnp.concatenate([upper, lower], axis=0)).reshape(4, 128, 256))
    part_ref[...] = shift_cols(sums[0], 1) + sums[1] + shift_cols(sums[2], -1)


def forward_kernel(near_ref, far_ref, own_ref, part_ref, w_ref, cot_ref, out_ref, grad_ref):
    even = lax.axis_index("space") % 2 == 0
    near, far = near_ref[...].reshape(4, 128, 256), far_ref[...].reshape(4, 128, 256)
    above, below = jnp.where(even, far, near), jnp.where(even, near, far)
    sums = []
    for c in range(3):
        upper = jnp.zeros((256, 256), jnp.float32)
        lower = jnp.zeros((256, 256), jnp.float32)
        for a in range(3):
            top = above[a : a + 2].reshape(256, 256)
            bottom = below[a : a + 2].reshape(256, 256)
            upper += jnp.dot(top, w_ref[a, 0, c], preferred_element_type=jnp.float32)
            lower += jnp.dot(bottom, w_ref[a, 1, c], preferred_element_type=jnp.float32)
        sums.append(jnp.concatenate([upper, lower], axis=0).reshape(4, 128, 256))
    total = part_ref[...] + shift_cols(sums[0], 1) + sums[1] + shift_cols(sums[2], -1)
    for row in range(2):
        preact = total[2 * row : 2 * row + 2]
        own = own_ref[:, row].astype(jnp.float32)
        sigma = 1.0 / (1.0 + jnp.exp(-preact))
        out_ref[:, row] = (own + preact * sigma).astype(jnp.bfloat16)
        cot = cot_ref[:, row].astype(jnp.float32)
        grad = cot * sigma * (1.0 + preact * (1.0 - sigma))
        grad_ref[:, row] = grad.astype(jnp.bfloat16)


def back_terms(tall_ref, w_ref, whole, single, source, to):
    sums = []
    for c in range(3):
        acc = jnp.zeros((512, 256), jnp.float32)
        one = jnp.zeros((256, 256), jnp.float32)
        for b in range(3):
            block = tall_ref[:, 2 - b : 4 - b]
            acc += lax.dot_general(
                block.reshape(512, 256),
                w_ref[whole, b, c],
                (((1,), (1,)), ((), ())),
                preferred_element_type=jnp.float32,
            )
            one += lax.dot_general(
                block[source].reshape(256, 256),
                w_ref[single, b, c],
                (((1,), (1,)), ((), ())),
                preferred_element_type=jnp.float32,
            )
        halves = [acc[:256], acc[256:]]
        halves[to] += one
        sums.append(jnp.concatenate(halves, axis=0).reshape(4, 128, 256))
    total = shift_cols(sums[0], -1) + sums[1] + shift_cols(sums[2], 1)
    return total.reshape(2, 2, 128, 256)


def earlier_kernel(tall_ref, w_from, out_ref, w_ref, sem):
    copy = pltpu.make_async_copy(w_from.at[0:2], w_ref, sem)
    copy.start()
    copy.wait()
    out_ref[...] = back_terms(tall_ref, w_ref, 0, 1, 0, 1).astype(jnp.bfloat16)


def backward_kernel(tall_ref, later_ref, w_from, cot_ref, out_ref, w_ref, sem):
    copy = pltpu.make_async_copy(w_from.at[1:3], w_ref, sem)
    copy.start()
    copy.wait()
    total = back_terms(tall_ref, w_ref, 1, 0, 1, 0) + later_ref[...].astype(jnp.float32)
    out_ref[...] = (cot_ref[...].astype(jnp.float32) + total).astype(jnp.bfloat16)


def call_back(kernel, n_before, n_after, flops):
    on_chip = pl.BlockSpec(memory_space=pltpu.VMEM)
    weights = pl.BlockSpec(memory_space=pltpu.HBM)
    return pl.pallas_call(
        kernel,
        out_shape=jax.ShapeDtypeStruct((2, 2, 128, 256), jnp.bfloat16),
        in_specs=[on_chip] * n_before + [weights] + [on_chip] * n_after,
        scratch_shapes=[pltpu.VMEM((2, 3, 3, 256, 256), jnp.bfloat16), pltpu.SemaphoreType.DMA],
        compiler_params=pltpu.CompilerParams(vmem_limit_bytes=50 * 1024 * 1024),
        cost_estimate=pl.CostEstimate(flops=flops, bytes_accessed=5000000, transcendentals=0),
    )


def turned_grad(grad_ref, order_ref):
    parts = []
    for steps in (-1, 0, 1):
        value = grad_ref[...].reshape(4, 128, 256)
        if steps:
            value = shift_cols(value.astype(jnp.float32), steps).astype(jnp.bfloat16)
        turned = lax.dot_general(
            order_ref[...],
            value.reshape(512, 256),
            (((1,), (1,)), ((), ())),
            preferred_element_type=jnp.float32,
        )
        parts.append(turned.astype(jnp.bfloat16))
    return jnp.concatenate(parts, axis=0)


TAPS = [(a, b) for a in range(3) for b in range(3)]


def own_terms_kernel(cells_ref, grad_ref, order_ref, out_ref):
    turned = turned_grad(grad_ref, order_ref)
    for start in range(0, 9, 2):
        some = TAPS[start : start + 2]
        cells = jnp.concatenate([block_of(cells_ref, a, b) for a, b in some], axis=1)
        out_ref[:, start * 128 : (start + len(some)) * 128] = jnp.dot(
            turned, cells, preferred_element_type=jnp.float32
        )


def terms_kernel(cells_ref, grad_ref, order_ref, part_ref, out_ref, held_ref, sems):
    turned = turned_grad(grad_ref, order_ref)
    copies = []
    for start in range(0, 9, 2):
        some = TAPS[start : start + 2]
        cells = jnp.concatenate([block_of(cells_ref, a, b) for a, b in some], axis=1)
        terms = jnp.dot(turned, cells, preferred_element_type=jnp.float32)
        terms += part_ref[:, start * 128 : (start + len(some)) * 128]
        terms = terms.astype(jnp.bfloat16)
        for i in range(len(some)):
            for c in range(3):
                tap = (start + i) * 3 + c
                held_ref[:, tap * 128 : (tap + 1) * 128] = terms[
                    c * 256 : (c + 1) * 256, i * 128 : (i + 1) * 128
                ]
        lanes = pl.ds(start * 384, len(some) * 384)
        copy = pltpu.make_async_copy(
            held_ref.at[:, lanes], out_ref.at[:, lanes], sems.at[start // 2]
        )
        copy.start()
        copies.append(copy)
    for copy in copies:
        copy.wait()


def plane_kernel(got_ref, out_ref):
    total = got_ref[0].astype(jnp.float32)
    for i in range(1, 16):
        total += got_ref[i].astype(jnp.float32)
    for z in range(8):
        out_ref[z] = total[2 * z : 2 * z + 2].astype(out_ref.dtype)


def line_kernel(got_ref, out_ref):
    total = got_ref[0].astype(jnp.float32)
    for i in range(1, 8):
        total += got_ref[i].astype(jnp.float32)
    total *= 1.0 / math.sqrt(32.0 * 32.0 * 128.0)
    for i in range(8):
        out_ref[i] = total


def share_kernel(mine_ref, other_ref, out_ref):
    core = lax.axis_index("tm") % 2
    for tap in range(27):
        lanes = slice(tap * 128, (tap + 1) * 128)
        mine = jnp.concatenate([mine_ref[q, :, lanes] for q in range(8)], axis=0)
        other = jnp.concatenate([other_ref[q, :, lanes] for q in range(8)], axis=0)
        out_ref[tap] = jnp.where(
            core == 0,
            jnp.concatenate([mine, other], axis=1),
            jnp.concatenate([other, mine], axis=1),
        )


def call(kernel, shapes, flops):
    return pl.pallas_call(
        kernel,
        out_shape=shapes,
        compiler_params=VMEM,
        cost_estimate=pl.CostEstimate(flops=flops, bytes_accessed=5000000, transcendentals=0),
    )


def row_order():
    channels = np.arange(256).reshape(2, 8, 8, 2).transpose(0, 2, 1, 3).reshape(256)
    return (channels[:, None] == np.arange(256)[None, :]).astype(np.float32)


def local(frames_in, weight, cotangent):
    core = lax.axis_index("tm") % 2
    block = jax.ShapeDtypeStruct((2, 2, 128, 256), jnp.bfloat16)
    flops = 2 * 512 * 6912 * 256

    carried = shifted(frames_in, "tm", 1)
    even = lax.axis_index("space") % 2 == 0
    edge = jax.ShapeDtypeStruct((2, 1, 128, 256), jnp.bfloat16)
    top, bottom, own = call(edge_kernel, (edge, edge, block), 100000)(frames_in)
    near, far = row_halo(
        jnp.concatenate([carried[:, :1], top], axis=0),
        jnp.concatenate([carried[:, 1:], bottom], axis=0),
    )
    part, held = call(
        near_kernel,
        (
            jax.ShapeDtypeStruct((4, 128, 256), jnp.float32),
            jax.ShapeDtypeStruct((3, 2, 3, 256, 256), jnp.bfloat16),
        ),
        flops,
    )(carried, own, weight)
    near, far, part = lax.optimization_barrier((near, far, part))
    output, grad_pre = call(forward_kernel, (block, block), flops // 3)(
        near, far, own, part, held, cotangent
    )
    near, far, grad_pre = lax.optimization_barrier((near, far, grad_pre))
    grad_other = flip_core(grad_pre)
    before, after = jnp.where(even, far, near), jnp.where(even, near, far)
    ext = jnp.concatenate(
        [before, jnp.concatenate([carried, own], axis=0), after], axis=1
    )
    low, high = ext[..., :128], ext[..., 128:]
    mine = jnp.where(core == 0, low, high)
    theirs = flip_core(jnp.where(core == 0, high, low))
    order = jnp.asarray(row_order(), jnp.bfloat16)
    own_terms = call(own_terms_kernel, jax.ShapeDtypeStruct((768, 1152), jnp.float32), flops // 2)(
        mine, grad_pre, order
    )
    terms = pl.pallas_call(
        terms_kernel,
        out_shape=jax.ShapeDtypeStruct((256, 3456), jnp.bfloat16),
        out_specs=pl.BlockSpec(memory_space=pl.ANY),
        scratch_shapes=[pltpu.VMEM((256, 3456), jnp.bfloat16), pltpu.SemaphoreType.DMA((5,))],
        compiler_params=VMEM,
        cost_estimate=pl.CostEstimate(flops=flops // 2, bytes_accessed=5000000, transcendentals=0),
    )(theirs, grad_other, order, own_terms)
    near, far = row_halo(grad_pre[:, :1], grad_pre[:, 1:])
    above, below = jnp.where(even, far, near), jnp.where(even, near, far)
    tall = jnp.concatenate([above, grad_pre, below], axis=1)
    earlier = call_back(earlier_kernel, 1, 0, flops // 2)(tall, weight)
    follow = shifted(earlier, "tm", -1)
    got = exchange(terms, ("x_lo", "x_hi", "y")).reshape(16, 16, 3456)
    plane = pl.pallas_call(
        plane_kernel,
        out_shape=jax.ShapeDtypeStruct((8, 2, 3456), jnp.bfloat16),
        grid=(3,),
        in_specs=[pl.BlockSpec((16, 16, 1152), lambda i: (0, 0, i))],
        out_specs=pl.BlockSpec((8, 2, 1152), lambda i: (0, 0, i)),
        compiler_params=VMEM,
    )(got)
    got = exchange(plane, ("z",)).reshape(8, 2, 3456)
    copies = call(line_kernel, jax.ShapeDtypeStruct((8, 2, 3456), jnp.float32), 100000)(got)
    copies, tall, follow = lax.optimization_barrier((copies, tall, follow))
    share = exchange(copies, ("x_hi", "y")).reshape(8, 2, 3456)
    grad_input = call_back(backward_kernel, 2, 1, flops // 2)(
        tall, follow, weight, cotangent
    )
    share, grad_input = lax.optimization_barrier((share, grad_input))
    other = flip_core(share)
    share = call(share_kernel, jax.ShapeDtypeStruct((27, 16, 256), jnp.float32), 100000)(
        share, other
    )
    grad_weight = share.transpose(1, 0, 2).reshape(16, 3, 3, 3, 256)
    return (output, grad_input, grad_weight)


def solution(mesh):
    placed = (P("tm", "space", None, None), P(), P("tm", "space", None, None))
    return jax.shard_map(
        local,
        mesh=mesh,
        in_specs=placed,
        out_specs=(
            P("tm", "space", None, None),
            P("tm", "space", None, None),
            P("space", None, None, None, None),
        ),
        check_vma=False,
    )
```

```python
import functools
import itertools
import math

import jax
import jax.numpy as jnp
import numpy as np
from jax import lax
from jax.experimental import pallas as pl
from jax.experimental.pallas import tpu as pltpu
from jax.sharding import PartitionSpec as P

BOTH = ("tm", "space")
VMEM = pltpu.CompilerParams(vmem_limit_bytes=20 * 1024 * 1024)
SIZES = {"x_hi": 2, "y": 4, "core": 2, "x_lo": 2, "z": 8}


def groups_of(names):
    rest = [n for n in SIZES if n not in names]
    groups = []
    for fixed in itertools.product(*(range(SIZES[n]) for n in rest)):
        group = []
        for varied in itertools.product(*(range(SIZES[n]) for n in names)):
            at = dict(zip(rest, fixed)) | dict(zip(names, varied))
            tm = (at["x_hi"] * 4 + at["y"]) * 2 + at["core"]
            group.append(tm * 16 + at["x_lo"] * 8 + at["z"])
        groups.append(group)
    return groups


Z_ORDER = (4, 5, 6, 7, 0, 1, 2, 3)


def exchange(value, names, order=None):
    groups = groups_of(names)
    if order:
        groups = [[group[i] for i in order] for group in groups]
    return lax.all_to_all(value, BOTH, 0, 0, tiled=True, axis_index_groups=groups)


def flip_core(value):
    return lax.ppermute(value, "tm", [(i, i ^ 1) for i in range(16)])


def shifted(value, axis, steps):
    count = lax.axis_size(axis)
    leading, last = (max(0, -steps), min(count, count - steps))
    return lax.ppermute(value, axis, [(source, source + steps) for source in range(leading, last)])


def pairs(value, first):
    links = [(i, i + 1) for i in range(first, 15, 2)]
    return lax.ppermute(value, "space", links + [(j, i) for i, j in links])


def row_halo(top, bottom):
    even = lax.axis_index("space") % 2 == 0
    near = pairs(jnp.where(even, bottom, top), 0)
    far = pairs(jnp.where(even, top, bottom), 1)
    return near, far


def shift_cols(value, steps):
    zero = jnp.zeros_like(value[:, :1])
    if steps == 1:
        return jnp.concatenate([zero, value[:, :-1]], axis=1)
    return jnp.concatenate([value[:, 1:], zero], axis=1)


def block_of(ref, a, b):
    return ref[a : a + 2, b : b + 2].reshape(512, -1)


def edge_kernel(frames_ref, top_ref, bottom_ref, own_ref):
    top_ref[...] = frames_ref[:, :1]
    bottom_ref[...] = frames_ref[:, 1:]
    own_ref[...] = frames_ref[...]


def near_kernel(carried_ref, own_ref, w_ref, part_ref, held_ref):
    held_ref[:, 0] = w_ref[:, 0]
    held_ref[:, 1] = w_ref[:, 2]
    blocks = [
        carried_ref[...],
        jnp.concatenate([carried_ref[1:], own_ref[:1]], axis=0),
        own_ref[...],
    ]
    sums = []
    for c in range(3):
        both = jnp.zeros((512, 256), jnp.float32)
        upper = jnp.zeros((256, 256), jnp.float32)
        lower = jnp.zeros((256, 256), jnp.float32)
        for a in range(3):
            rows = [blocks[a][:, r].reshape(256, 256) for r in range(2)]
            both += jnp.dot(
                jnp.concatenate(rows, axis=0), w_ref[a, 1, c], preferred_element_type=jnp.float32
            )
            upper += jnp.dot(rows[1], w_ref[a, 2, c], preferred_element_type=jnp.float32)
            lower += jnp.dot(rows[0], w_ref[a, 0, c], preferred_element_type=jnp.float32)
        sums.append((both + jnp.concatenate([upper, lower], axis=0)).reshape(4, 128, 256))
    part_ref[...] = shift_cols(sums[0], 1) + sums[1] + shift_cols(sums[2], -1)


def forward_kernel(near_ref, far_ref, own_ref, part_ref, w_ref, cot_ref, out_ref, grad_ref):
    even = lax.axis_index("space") % 2 == 0
    near, far = near_ref[...].reshape(4, 128, 256), far_ref[...].reshape(4, 128, 256)
    above, below = jnp.where(even, far, near), jnp.where(even, near, far)
    sums = []
    for c in range(3):
        upper = jnp.zeros((256, 256), jnp.float32)
        lower = jnp.zeros((256, 256), jnp.float32)
        for a in range(3):
            top = above[a : a + 2].reshape(256, 256)
            bottom = below[a : a + 2].reshape(256, 256)
            upper += jnp.dot(top, w_ref[a, 0, c], preferred_element_type=jnp.float32)
            lower += jnp.dot(bottom, w_ref[a, 1, c], preferred_element_type=jnp.float32)
        sums.append(jnp.concatenate([upper, lower], axis=0).reshape(4, 128, 256))
    total = part_ref[...] + shift_cols(sums[0], 1) + sums[1] + shift_cols(sums[2], -1)
    for row in range(2):
        preact = total[2 * row : 2 * row + 2]
        own = own_ref[:, row].astype(jnp.float32)
        sigma = 1.0 / (1.0 + jnp.exp(-preact))
        out_ref[:, row] = (own + preact * sigma).astype(jnp.bfloat16)
        cot = cot_ref[:, row].astype(jnp.float32)
        grad = cot * sigma * (1.0 + preact * (1.0 - sigma))
        grad_ref[:, row] = grad.astype(jnp.bfloat16)


def back_terms(tall_ref, w_ref, whole, single, source, to):
    sums = []
    for c in range(3):
        acc = jnp.zeros((512, 256), jnp.float32)
        one = jnp.zeros((256, 256), jnp.float32)
        for b in range(3):
            block = tall_ref[:, 2 - b : 4 - b]
            acc += lax.dot_general(
                block.reshape(512, 256),
                w_ref[whole, b, c],
                (((1,), (1,)), ((), ())),
                preferred_element_type=jnp.float32,
            )
            one += lax.dot_general(
                block[source].reshape(256, 256),
                w_ref[single, b, c],
                (((1,), (1,)), ((), ())),
                preferred_element_type=jnp.float32,
            )
        halves = [acc[:256], acc[256:]]
        halves[to] += one
        sums.append(jnp.concatenate(halves, axis=0).reshape(4, 128, 256))
    total = shift_cols(sums[0], -1) + sums[1] + shift_cols(sums[2], 1)
    return total.reshape(2, 2, 128, 256)


def earlier_kernel(tall_ref, w_from, out_ref, w_ref, sem):
    copy = pltpu.make_async_copy(w_from.at[0:2], w_ref, sem)
    copy.start()
    copy.wait()
    out_ref[...] = back_terms(tall_ref, w_ref, 0, 1, 0, 1).astype(jnp.bfloat16)


def backward_kernel(tall_ref, later_ref, w_from, cot_ref, out_ref, w_ref, sem):
    copy = pltpu.make_async_copy(w_from.at[1:3], w_ref, sem)
    copy.start()
    copy.wait()
    total = back_terms(tall_ref, w_ref, 1, 0, 1, 0) + later_ref[...].astype(jnp.float32)
    out_ref[...] = (cot_ref[...].astype(jnp.float32) + total).astype(jnp.bfloat16)


def call_back(kernel, n_before, n_after, flops):
    on_chip = pl.BlockSpec(memory_space=pltpu.VMEM)
    weights = pl.BlockSpec(memory_space=pltpu.HBM)
    return pl.pallas_call(
        kernel,
        out_shape=jax.ShapeDtypeStruct((2, 2, 128, 256), jnp.bfloat16),
        in_specs=[on_chip] * n_before + [weights] + [on_chip] * n_after,
        scratch_shapes=[pltpu.VMEM((2, 3, 3, 256, 256), jnp.bfloat16), pltpu.SemaphoreType.DMA],
        compiler_params=pltpu.CompilerParams(vmem_limit_bytes=50 * 1024 * 1024),
        cost_estimate=pl.CostEstimate(flops=flops, bytes_accessed=5000000, transcendentals=0),
    )


def turned_grad(grad_ref, order_ref):
    parts = []
    for steps in (-1, 0, 1):
        value = grad_ref[...].reshape(4, 128, 256)
        if steps:
            value = shift_cols(value.astype(jnp.float32), steps).astype(jnp.bfloat16)
        turned = lax.dot_general(
            order_ref[...],
            value.reshape(512, 256),
            (((1,), (1,)), ((), ())),
            preferred_element_type=jnp.float32,
        )
        parts.append(turned.astype(jnp.bfloat16))
    return jnp.concatenate(parts, axis=0)


TAPS = [(a, b) for a in range(3) for b in range(3)]


def own_terms_kernel(cells_ref, grad_ref, order_ref, out_ref):
    turned = turned_grad(grad_ref, order_ref)
    for start in range(0, 9, 2):
        some = TAPS[start : start + 2]
        cells = jnp.concatenate([block_of(cells_ref, a, b) for a, b in some], axis=1)
        out_ref[:, start * 128 : (start + len(some)) * 128] = jnp.dot(
            turned, cells, preferred_element_type=jnp.float32
        )


def terms_kernel(cells_ref, grad_ref, order_ref, part_ref, out_ref, held_ref, sems):
    turned = turned_grad(grad_ref, order_ref)
    copies = []
    for start in range(0, 9, 2):
        some = TAPS[start : start + 2]
        cells = jnp.concatenate([block_of(cells_ref, a, b) for a, b in some], axis=1)
        terms = jnp.dot(turned, cells, preferred_element_type=jnp.float32)
        terms += part_ref[:, start * 128 : (start + len(some)) * 128]
        terms = terms.astype(jnp.bfloat16)
        for i in range(len(some)):
            for c in range(3):
                tap = (start + i) * 3 + c
                held_ref[:, tap * 128 : (tap + 1) * 128] = terms[
                    c * 256 : (c + 1) * 256, i * 128 : (i + 1) * 128
                ]
        lanes = pl.ds(start * 384, len(some) * 384)
        copy = pltpu.make_async_copy(
            held_ref.at[:, lanes], out_ref.at[:, lanes], sems.at[start // 2]
        )
        copy.start()
        copies.append(copy)
    for copy in copies:
        copy.wait()


def plane_kernel(got_ref, out_ref):
    total = got_ref[0].astype(jnp.float32)
    for i in range(1, 16):
        total += got_ref[i].astype(jnp.float32)
    for at, z in enumerate(Z_ORDER):
        out_ref[at] = total[2 * z : 2 * z + 2].astype(out_ref.dtype)


def line_kernel(got_ref, out_ref):
    total = got_ref[0].astype(jnp.float32)
    for i in range(1, 8):
        total += got_ref[i].astype(jnp.float32)
    total *= 1.0 / math.sqrt(32.0 * 32.0 * 128.0)
    for i in range(8):
        out_ref[i] = total


def share_kernel(mine_ref, other_ref, out_ref):
    core = lax.axis_index("tm") % 2
    for tap in range(27):
        lanes = slice(tap * 128, (tap + 1) * 128)
        mine = jnp.concatenate([mine_ref[q, :, lanes] for q in range(8)], axis=0)
        other = jnp.concatenate([other_ref[q, :, lanes] for q in range(8)], axis=0)
        out_ref[tap] = jnp.where(
            core == 0,
            jnp.concatenate([mine, other], axis=1),
            jnp.concatenate([other, mine], axis=1),
        )


def call(kernel, shapes, flops):
    return pl.pallas_call(
        kernel,
        out_shape=shapes,
        compiler_params=VMEM,
        cost_estimate=pl.CostEstimate(flops=flops, bytes_accessed=5000000, transcendentals=0),
    )


def row_order():
    channels = np.arange(256).reshape(2, 8, 8, 2).transpose(0, 2, 1, 3).reshape(256)
    return (channels[:, None] == np.arange(256)[None, :]).astype(np.float32)


def local(frames_in, weight, cotangent):
    core = lax.axis_index("tm") % 2
    block = jax.ShapeDtypeStruct((2, 2, 128, 256), jnp.bfloat16)
    flops = 2 * 512 * 6912 * 256

    carried = shifted(frames_in, "tm", 1)
    even = lax.axis_index("space") % 2 == 0
    edge = jax.ShapeDtypeStruct((2, 1, 128, 256), jnp.bfloat16)
    top, bottom, own = call(edge_kernel, (edge, edge, block), 100000)(frames_in)
    near, far = row_halo(
        jnp.concatenate([carried[:, :1], top], axis=0),
        jnp.concatenate([carried[:, 1:], bottom], axis=0),
    )
    part, held = call(
        near_kernel,
        (
            jax.ShapeDtypeStruct((4, 128, 256), jnp.float32),
            jax.ShapeDtypeStruct((3, 2, 3, 256, 256), jnp.bfloat16),
        ),
        flops,
    )(carried, own, weight)
    near, far, part = lax.optimization_barrier((near, far, part))
    output, grad_pre = call(forward_kernel, (block, block), flops // 3)(
        near, far, own, part, held, cotangent
    )
    near, far, grad_pre = lax.optimization_barrier((near, far, grad_pre))
    grad_other = flip_core(grad_pre)
    before, after = jnp.where(even, far, near), jnp.where(even, near, far)
    ext = jnp.concatenate(
        [before, jnp.concatenate([carried, own], axis=0), after], axis=1
    )
    low, high = ext[..., :128], ext[..., 128:]
    mine = jnp.where(core == 0, low, high)
    theirs = flip_core(jnp.where(core == 0, high, low))
    order = jnp.asarray(row_order(), jnp.bfloat16)
    own_terms = call(own_terms_kernel, jax.ShapeDtypeStruct((768, 1152), jnp.float32), flops // 2)(
        mine, grad_pre, order
    )
    terms = pl.pallas_call(
        terms_kernel,
        out_shape=jax.ShapeDtypeStruct((256, 3456), jnp.bfloat16),
        out_specs=pl.BlockSpec(memory_space=pl.ANY),
        scratch_shapes=[pltpu.VMEM((256, 3456), jnp.bfloat16), pltpu.SemaphoreType.DMA((5,))],
        compiler_params=VMEM,
        cost_estimate=pl.CostEstimate(flops=flops // 2, bytes_accessed=5000000, transcendentals=0),
    )(theirs, grad_other, order, own_terms)
    near, far = row_halo(grad_pre[:, :1], grad_pre[:, 1:])
    above, below = jnp.where(even, far, near), jnp.where(even, near, far)
    tall = jnp.concatenate([above, grad_pre, below], axis=1)
    earlier = call_back(earlier_kernel, 1, 0, flops // 2)(tall, weight)
    follow = shifted(earlier, "tm", -1)
    got = exchange(terms, ("x_lo", "x_hi", "y")).reshape(16, 16, 3456)
    plane = pl.pallas_call(
        plane_kernel,
        out_shape=jax.ShapeDtypeStruct((8, 2, 3456), jnp.bfloat16),
        grid=(3,),
        in_specs=[pl.BlockSpec((16, 16, 1152), lambda i: (0, 0, i))],
        out_specs=pl.BlockSpec((8, 2, 1152), lambda i: (0, 0, i)),
        compiler_params=VMEM,
    )(got)
    got = exchange(plane, ("z",), Z_ORDER).reshape(8, 2, 3456)
    copies = call(line_kernel, jax.ShapeDtypeStruct((8, 2, 3456), jnp.float32), 100000)(got)
    copies, tall, follow = lax.optimization_barrier((copies, tall, follow))
    share = exchange(copies, ("x_hi", "y")).reshape(8, 2, 3456)
    grad_input = call_back(backward_kernel, 2, 1, flops // 2)(
        tall, follow, weight, cotangent
    )
    share, grad_input = lax.optimization_barrier((share, grad_input))
    other = flip_core(share)
    share = call(share_kernel, jax.ShapeDtypeStruct((27, 16, 256), jnp.float32), 100000)(
        share, other
    )
    grad_weight = share.transpose(1, 0, 2).reshape(16, 3, 3, 3, 256)
    return (output, grad_input, grad_weight)


def solution(mesh):
    placed = (P("tm", "space", None, None), P(), P("tm", "space", None, None))
    return jax.shard_map(
        local,
        mesh=mesh,
        in_specs=placed,
        out_specs=(
            P("tm", "space", None, None),
            P("tm", "space", None, None),
            P("space", None, None, None, None),
        ),
        check_vma=False,
    )
```

```python
import functools
import itertools
import math

import jax
import jax.numpy as jnp
import numpy as np
from jax import lax
from jax.experimental import pallas as pl
from jax.experimental.pallas import tpu as pltpu
from jax.sharding import PartitionSpec as P

BOTH = ("tm", "space")
VMEM = pltpu.CompilerParams(vmem_limit_bytes=20 * 1024 * 1024)
SIZES = {"x_hi": 2, "y": 4, "core": 2, "x_lo": 2, "z": 8}


def groups_of(names):
    rest = [n for n in SIZES if n not in names]
    groups = []
    for fixed in itertools.product(*(range(SIZES[n]) for n in rest)):
        group = []
        for varied in itertools.product(*(range(SIZES[n]) for n in names)):
            at = dict(zip(rest, fixed)) | dict(zip(names, varied))
            tm = (at["x_hi"] * 4 + at["y"]) * 2 + at["core"]
            group.append(tm * 16 + at["x_lo"] * 8 + at["z"])
        groups.append(group)
    return groups


Z_ORDER = (4, 5, 6, 7, 0, 1, 2, 3)
SHARE_ORDER = (7, 6, 5, 4, 3, 2, 1, 0)


def exchange(value, names, order=None):
    groups = groups_of(names)
    if order:
        groups = [[group[i] for i in order] for group in groups]
    return lax.all_to_all(value, BOTH, 0, 0, tiled=True, axis_index_groups=groups)


def flip_core(value):
    return lax.ppermute(value, "tm", [(i, i ^ 1) for i in range(16)])


def shifted(value, axis, steps):
    count = lax.axis_size(axis)
    leading, last = (max(0, -steps), min(count, count - steps))
    return lax.ppermute(value, axis, [(source, source + steps) for source in range(leading, last)])


def pairs(value, first):
    links = [(i, i + 1) for i in range(first, 15, 2)]
    return lax.ppermute(value, "space", links + [(j, i) for i, j in links])


def row_halo(top, bottom):
    even = lax.axis_index("space") % 2 == 0
    near = pairs(jnp.where(even, bottom, top), 0)
    far = pairs(jnp.where(even, top, bottom), 1)
    return near, far


def shift_cols(value, steps):
    zero = jnp.zeros_like(value[:, :1])
    if steps == 1:
        return jnp.concatenate([zero, value[:, :-1]], axis=1)
    return jnp.concatenate([value[:, 1:], zero], axis=1)


def block_of(ref, a, b):
    return ref[a : a + 2, b : b + 2].reshape(512, -1)


def edge_kernel(frames_ref, top_ref, bottom_ref, own_ref):
    top_ref[...] = frames_ref[:, :1]
    bottom_ref[...] = frames_ref[:, 1:]
    own_ref[...] = frames_ref[...]


def near_kernel(carried_ref, own_ref, w_ref, part_ref, held_ref):
    held_ref[:, 0] = w_ref[:, 0]
    held_ref[:, 1] = w_ref[:, 2]
    blocks = [
        carried_ref[...],
        jnp.concatenate([carried_ref[1:], own_ref[:1]], axis=0),
        own_ref[...],
    ]
    sums = []
    for c in range(3):
        both = jnp.zeros((512, 256), jnp.float32)
        upper = jnp.zeros((256, 256), jnp.float32)
        lower = jnp.zeros((256, 256), jnp.float32)
        for a in range(3):
            rows = [blocks[a][:, r].reshape(256, 256) for r in range(2)]
            both += jnp.dot(
                jnp.concatenate(rows, axis=0), w_ref[a, 1, c], preferred_element_type=jnp.float32
            )
            upper += jnp.dot(rows[1], w_ref[a, 2, c], preferred_element_type=jnp.float32)
            lower += jnp.dot(rows[0], w_ref[a, 0, c], preferred_element_type=jnp.float32)
        sums.append((both + jnp.concatenate([upper, lower], axis=0)).reshape(4, 128, 256))
    part_ref[...] = shift_cols(sums[0], 1) + sums[1] + shift_cols(sums[2], -1)


def forward_kernel(near_ref, far_ref, own_ref, part_ref, w_ref, cot_ref, out_ref, grad_ref):
    even = lax.axis_index("space") % 2 == 0
    near, far = near_ref[...].reshape(4, 128, 256), far_ref[...].reshape(4, 128, 256)
    above, below = jnp.where(even, far, near), jnp.where(even, near, far)
    sums = []
    for c in range(3):
        upper = jnp.zeros((256, 256), jnp.float32)
        lower = jnp.zeros((256, 256), jnp.float32)
        for a in range(3):
            top = above[a : a + 2].reshape(256, 256)
            bottom = below[a : a + 2].reshape(256, 256)
            upper += jnp.dot(top, w_ref[a, 0, c], preferred_element_type=jnp.float32)
            lower += jnp.dot(bottom, w_ref[a, 1, c], preferred_element_type=jnp.float32)
        sums.append(jnp.concatenate([upper, lower], axis=0).reshape(4, 128, 256))
    total = part_ref[...] + shift_cols(sums[0], 1) + sums[1] + shift_cols(sums[2], -1)
    for row in range(2):
        preact = total[2 * row : 2 * row + 2]
        own = own_ref[:, row].astype(jnp.float32)
        sigma = 1.0 / (1.0 + jnp.exp(-preact))
        out_ref[:, row] = (own + preact * sigma).astype(jnp.bfloat16)
        cot = cot_ref[:, row].astype(jnp.float32)
        grad = cot * sigma * (1.0 + preact * (1.0 - sigma))
        grad_ref[:, row] = grad.astype(jnp.bfloat16)


def back_terms(tall_ref, w_ref, whole, single, source, to):
    sums = []
    for c in range(3):
        acc = jnp.zeros((512, 256), jnp.float32)
        one = jnp.zeros((256, 256), jnp.float32)
        for b in range(3):
            block = tall_ref[:, 2 - b : 4 - b]
            acc += lax.dot_general(
                block.reshape(512, 256),
                w_ref[whole, b, c],
                (((1,), (1,)), ((), ())),
                preferred_element_type=jnp.float32,
            )
            one += lax.dot_general(
                block[source].reshape(256, 256),
                w_ref[single, b, c],
                (((1,), (1,)), ((), ())),
                preferred_element_type=jnp.float32,
            )
        halves = [acc[:256], acc[256:]]
        halves[to] += one
        sums.append(jnp.concatenate(halves, axis=0).reshape(4, 128, 256))
    total = shift_cols(sums[0], -1) + sums[1] + shift_cols(sums[2], 1)
    return total.reshape(2, 2, 128, 256)


def earlier_kernel(tall_ref, w_from, out_ref, w_ref, sem):
    copy = pltpu.make_async_copy(w_from.at[0:2], w_ref, sem)
    copy.start()
    copy.wait()
    out_ref[...] = back_terms(tall_ref, w_ref, 0, 1, 0, 1).astype(jnp.bfloat16)


def backward_kernel(tall_ref, later_ref, w_from, cot_ref, out_ref, w_ref, sem):
    copy = pltpu.make_async_copy(w_from.at[1:3], w_ref, sem)
    copy.start()
    copy.wait()
    total = back_terms(tall_ref, w_ref, 1, 0, 1, 0) + later_ref[...].astype(jnp.float32)
    out_ref[...] = (cot_ref[...].astype(jnp.float32) + total).astype(jnp.bfloat16)


def call_back(kernel, n_before, n_after, flops):
    on_chip = pl.BlockSpec(memory_space=pltpu.VMEM)
    weights = pl.BlockSpec(memory_space=pltpu.HBM)
    return pl.pallas_call(
        kernel,
        out_shape=jax.ShapeDtypeStruct((2, 2, 128, 256), jnp.bfloat16),
        in_specs=[on_chip] * n_before + [weights] + [on_chip] * n_after,
        scratch_shapes=[pltpu.VMEM((2, 3, 3, 256, 256), jnp.bfloat16), pltpu.SemaphoreType.DMA],
        compiler_params=pltpu.CompilerParams(vmem_limit_bytes=50 * 1024 * 1024),
        cost_estimate=pl.CostEstimate(flops=flops, bytes_accessed=5000000, transcendentals=0),
    )


def turned_grad(grad_ref, order_ref):
    parts = []
    for steps in (-1, 0, 1):
        value = grad_ref[...].reshape(4, 128, 256)
        if steps:
            value = shift_cols(value.astype(jnp.float32), steps).astype(jnp.bfloat16)
        turned = lax.dot_general(
            order_ref[...],
            value.reshape(512, 256),
            (((1,), (1,)), ((), ())),
            preferred_element_type=jnp.float32,
        )
        parts.append(turned.astype(jnp.bfloat16))
    return jnp.concatenate(parts, axis=0)


TAPS = [(a, b) for a in range(3) for b in range(3)]


def own_terms_kernel(cells_ref, grad_ref, order_ref, out_ref):
    turned = turned_grad(grad_ref, order_ref)
    for start in range(0, 9, 2):
        some = TAPS[start : start + 2]
        cells = jnp.concatenate([block_of(cells_ref, a, b) for a, b in some], axis=1)
        out_ref[:, start * 128 : (start + len(some)) * 128] = jnp.dot(
            turned, cells, preferred_element_type=jnp.float32
        )


def terms_kernel(cells_ref, grad_ref, order_ref, part_ref, out_ref, held_ref, sems):
    turned = turned_grad(grad_ref, order_ref)
    copies = []
    for start in range(0, 9, 2):
        some = TAPS[start : start + 2]
        cells = jnp.concatenate([block_of(cells_ref, a, b) for a, b in some], axis=1)
        terms = jnp.dot(turned, cells, preferred_element_type=jnp.float32)
        terms += part_ref[:, start * 128 : (start + len(some)) * 128]
        terms = terms.astype(jnp.bfloat16)
        for i in range(len(some)):
            for c in range(3):
                tap = (start + i) * 3 + c
                held_ref[:, tap * 128 : (tap + 1) * 128] = terms[
                    c * 256 : (c + 1) * 256, i * 128 : (i + 1) * 128
                ]
        lanes = pl.ds(start * 384, len(some) * 384)
        copy = pltpu.make_async_copy(
            held_ref.at[:, lanes], out_ref.at[:, lanes], sems.at[start // 2]
        )
        copy.start()
        copies.append(copy)
    for copy in copies:
        copy.wait()


def plane_kernel(got_ref, out_ref):
    total = got_ref[0].astype(jnp.float32)
    for i in range(1, 16):
        total += got_ref[i].astype(jnp.float32)
    for at, z in enumerate(Z_ORDER):
        out_ref[at] = total[2 * z : 2 * z + 2].astype(out_ref.dtype)


def line_kernel(got_ref, out_ref):
    total = got_ref[0].astype(jnp.float32)
    for i in range(1, 8):
        total += got_ref[i].astype(jnp.float32)
    total *= 1.0 / math.sqrt(32.0 * 32.0 * 128.0)
    for i in range(8):
        out_ref[i] = total


def share_kernel(mine_ref, other_ref, out_ref):
    core = lax.axis_index("tm") % 2
    for tap in range(27):
        lanes = slice(tap * 128, (tap + 1) * 128)
        mine = jnp.concatenate([mine_ref[SHARE_ORDER.index(q), :, lanes] for q in range(8)], axis=0)
        other = jnp.concatenate([other_ref[SHARE_ORDER.index(q), :, lanes] for q in range(8)], axis=0)
        out_ref[tap] = jnp.where(
            core == 0,
            jnp.concatenate([mine, other], axis=1),
            jnp.concatenate([other, mine], axis=1),
        )


def call(kernel, shapes, flops):
    return pl.pallas_call(
        kernel,
        out_shape=shapes,
        compiler_params=VMEM,
        cost_estimate=pl.CostEstimate(flops=flops, bytes_accessed=5000000, transcendentals=0),
    )


def row_order():
    channels = np.arange(256).reshape(2, 8, 8, 2).transpose(0, 2, 1, 3).reshape(256)
    return (channels[:, None] == np.arange(256)[None, :]).astype(np.float32)


def local(frames_in, weight, cotangent):
    core = lax.axis_index("tm") % 2
    block = jax.ShapeDtypeStruct((2, 2, 128, 256), jnp.bfloat16)
    flops = 2 * 512 * 6912 * 256

    carried = shifted(frames_in, "tm", 1)
    even = lax.axis_index("space") % 2 == 0
    edge = jax.ShapeDtypeStruct((2, 1, 128, 256), jnp.bfloat16)
    top, bottom, own = call(edge_kernel, (edge, edge, block), 100000)(frames_in)
    near, far = row_halo(
        jnp.concatenate([carried[:, :1], top], axis=0),
        jnp.concatenate([carried[:, 1:], bottom], axis=0),
    )
    part, held = call(
        near_kernel,
        (
            jax.ShapeDtypeStruct((4, 128, 256), jnp.float32),
            jax.ShapeDtypeStruct((3, 2, 3, 256, 256), jnp.bfloat16),
        ),
        flops,
    )(carried, own, weight)
    near, far, part = lax.optimization_barrier((near, far, part))
    output, grad_pre = call(forward_kernel, (block, block), flops // 3)(
        near, far, own, part, held, cotangent
    )
    near, far, grad_pre = lax.optimization_barrier((near, far, grad_pre))
    grad_other = flip_core(grad_pre)
    before, after = jnp.where(even, far, near), jnp.where(even, near, far)
    ext = jnp.concatenate(
        [before, jnp.concatenate([carried, own], axis=0), after], axis=1
    )
    low, high = ext[..., :128], ext[..., 128:]
    mine = jnp.where(core == 0, low, high)
    theirs = flip_core(jnp.where(core == 0, high, low))
    order = jnp.asarray(row_order(), jnp.bfloat16)
    own_terms = call(own_terms_kernel, jax.ShapeDtypeStruct((768, 1152), jnp.float32), flops // 2)(
        mine, grad_pre, order
    )
    terms = pl.pallas_call(
        terms_kernel,
        out_shape=jax.ShapeDtypeStruct((256, 3456), jnp.bfloat16),
        out_specs=pl.BlockSpec(memory_space=pl.ANY),
        scratch_shapes=[pltpu.VMEM((256, 3456), jnp.bfloat16), pltpu.SemaphoreType.DMA((5,))],
        compiler_params=VMEM,
        cost_estimate=pl.CostEstimate(flops=flops // 2, bytes_accessed=5000000, transcendentals=0),
    )(theirs, grad_other, order, own_terms)
    near, far = row_halo(grad_pre[:, :1], grad_pre[:, 1:])
    above, below = jnp.where(even, far, near), jnp.where(even, near, far)
    tall = jnp.concatenate([above, grad_pre, below], axis=1)
    earlier = call_back(earlier_kernel, 1, 0, flops // 2)(tall, weight)
    follow = shifted(earlier, "tm", -1)
    got = exchange(terms, ("x_lo", "x_hi", "y")).reshape(16, 16, 3456)
    plane = pl.pallas_call(
        plane_kernel,
        out_shape=jax.ShapeDtypeStruct((8, 2, 3456), jnp.bfloat16),
        grid=(3,),
        in_specs=[pl.BlockSpec((16, 16, 1152), lambda i: (0, 0, i))],
        out_specs=pl.BlockSpec((8, 2, 1152), lambda i: (0, 0, i)),
        compiler_params=VMEM,
    )(got)
    got = exchange(plane, ("z",), Z_ORDER).reshape(8, 2, 3456)
    copies = call(line_kernel, jax.ShapeDtypeStruct((8, 2, 3456), jnp.float32), 100000)(got)
    copies, tall, follow = lax.optimization_barrier((copies, tall, follow))
    share = exchange(copies, ("x_hi", "y"), SHARE_ORDER).reshape(8, 2, 3456)
    grad_input = call_back(backward_kernel, 2, 1, flops // 2)(
        tall, follow, weight, cotangent
    )
    share, grad_input = lax.optimization_barrier((share, grad_input))
    other = flip_core(share)
    share = call(share_kernel, jax.ShapeDtypeStruct((27, 16, 256), jnp.float32), 100000)(
        share, other
    )
    grad_weight = share.transpose(1, 0, 2).reshape(16, 3, 3, 3, 256)
    return (output, grad_input, grad_weight)


def solution(mesh):
    placed = (P("tm", "space", None, None), P(), P("tm", "space", None, None))
    return jax.shard_map(
        local,
        mesh=mesh,
        in_specs=placed,
        out_specs=(
            P("tm", "space", None, None),
            P("tm", "space", None, None),
            P("space", None, None, None, None),
        ),
        check_vma=False,
    )
```
